256 devices in a mesh: row: 8 (over z), col: 32 (over x, y, core).
Axes of the slice: x: 4, y: 4, z: 8, core: 2. Of those that a mesh axis runs over, the one named last changes fastest.
Arguments:
- xn: bfloat16 [1024, 2048], P('col', 'row'), may hold values from -6 to 6
- w_qkv: bfloat16 [2048, 6144], P('row', 'col'), may hold values from -0.125 to 0.125
- w_out: bfloat16 [2048, 2048], P('col', 'row'), may hold values from -0.125 to 0.125
- pool: bfloat16 [2048, 64, 4096], P('row', None, 'col'), may hold values from -136 to 136
- page_table: int32 [1024, 64], P('row'), may hold values from 0 to 271
- lengths: int32 [1024], P('row'), may hold values from 1 to 4096, 98304 in all
- mig_src: int32 [128], replicated, may hold values from 0 to 2047, as said below
- deal: int32 [1024], replicated, may hold values from 0 to 1023, each once
Outputs:
- attended: bfloat16 [1024, 2048], P('col', 'row')
- landed: bfloat16 [128, 64, 4096], P('row', None, 'col')
The draws below stay inside these ranges and needn't reach their ends.
Inputs may be any that keep to these rules, and one draw needn't show every extreme that they name: `page_table`: page ids of a request refer to its own row block: below 256 its pool pages, from 256 its landing slots. `lengths`: the longest request has exactly 4096 cache tokens. `mig_src`: slot d belongs to row block d // 16; its source page lies in the pool pages of another row block. `deal`: a permutation of the requests.
All inputs are finite; a program needn't handle non-finite values. No bound on the sum of `lengths` on one device may be relied on, other than what follows from the above.
Results may differ from the reference program's by a relative error of at most 0.02.
Values may be sent and summed in bfloat16 or wider, within the bound.
A program may use at most 128 MiB of HBM per device.

```python
import math
import jax
import jax.numpy as jnp
import numpy as np
from jax import lax

D = 2048
HEADS = 32
HEAD_DIM = 64
REQUESTS = 1024
REQ_ROW = 128
PAGE = 64
MAXLEN = 4096
MAXP = 64
MEAN_LEN = 96
POOL_DEV = 256
LAND_DEV = 16
POOL = 2048
LANDING = 128


def draw_pool(key, part):
    shape = (POOL, PAGE, 2 * D)
    base = jnp.clip(jax.random.normal(jax.random.fold_in(key, 13), shape, jnp.float32), -6.0, 6.0)
    return base.astype(jnp.bfloat16)


def draw_mig_src(key, part):
    slots = jnp.arange(LANDING, dtype=jnp.int32)
    blocks = LANDING // LAND_DEV
    target = slots // LAND_DEV
    first_key, second_key = jax.random.split(jax.random.fold_in(key, 7))
    offset = jax.random.randint(first_key, (LANDING,), 1, blocks, dtype=jnp.int32)
    source_block = (target + offset) % blocks
    page_no = jax.random.randint(second_key, (LANDING,), 0, POOL_DEV, dtype=jnp.int32)
    return (source_block * POOL_DEV + page_no).astype(jnp.int32)


def touch_ends(result, rng, least, high):
    longest = result.shape.index(max(result.shape))
    spots = []
    for shift in (0, 1):
        where = [jax.random.randint(jax.random.fold_in(rng, axis), (), 0, length) for axis, length in enumerate(result.shape)]
        where[longest] = (where[longest] + shift) % result.shape[longest]
        spots.append(tuple(where))
    return result.at[spots[0]].set(least).at[spots[1]].set(high)


def levels(own_key, extent, cuts, low, high):
    level, own = 1.0, jax.random.fold_in(own_key, 6)
    for axis_at, blocks in cuts:
        heights = jnp.exp(jax.random.uniform(jax.random.fold_in(own, axis_at), (blocks,), jnp.float32, low / len(cuts), high / len(cuts)))
        level = level * jnp.repeat(heights, extent[axis_at] // blocks).reshape([-1 if axis == axis_at else 1 for axis in range(len(extent))])
    return level


def length_profile(number_of, total, limit, slope):
    weights = [(1 << 20) // math.isqrt(standing ** slope) + 1 for standing in range(2, number_of + 1)]
    spare, given = total - limit - (number_of - 1), [1] * (number_of - 1)
    while spare > 0:
        free = [i for i in range(number_of - 1) if given[i] < limit]
        mass, remaining = sum([weights[i] for i in free]), spare
        for i in free:
            more = min(limit - given[i], max(1, remaining * weights[i] // mass), spare)
            given[i] = given[i] + more
            spare = spare - more
    return np.array([limit] + given)


def ragged(stream_key, number_of, total, most, skew):
    if number_of == 2:
        one = jax.random.randint(stream_key, (), max(1, total - most), min(most, total - 1) + 1)
        return jnp.stack([one, total - one])
    sizes = jnp.asarray(length_profile(number_of, total, most, skew), jnp.int32)
    twos = (number_of - 1) // 2
    source_of, taker = sizes[1:1 + 2 * twos:2], sizes[2:2 + 2 * twos:2]
    room = jnp.minimum(source_of - 1, most - taker)
    passed = jax.random.randint(jax.random.fold_in(stream_key, 1), (twos,), 0, 1 << 20) % (room + 1)
    sizes = sizes.at[1:1 + 2 * twos:2].set(source_of - passed).at[2:2 + 2 * twos:2].set(taker + passed)
    return sizes[jax.random.permutation(jax.random.fold_in(stream_key, 2), number_of)]


def scatter_about(stream_key, extent, spread, most, cuts=(), kind=jnp.bfloat16):
    values = spread * jax.random.normal(stream_key, extent, jnp.float32)
    if cuts:
        values = values * levels(stream_key, extent, cuts, -0.22, 0.18)
    return jnp.clip(values, -most, most).astype(kind)


def setup_inputs(seed: int = 0) -> dict:
    arg_keys = jax.random.split(jax.random.key(seed), 9)
    return {
        "xn": scatter_about(arg_keys[0], (REQUESTS, D), 1.0, 6.0, ((0, 32), (1, 8))),
        "w_qkv": scatter_about(arg_keys[1], (D, 3 * D), D ** -0.5, 0.125, ((0, 8), (1, 32))),
        "w_out": scatter_about(arg_keys[2], (D, D), D ** -0.5, 0.125, ((0, 32), (1, 8))),
        "pool": draw_pool(jax.random.fold_in(arg_keys[8], 71), 0),
        "page_table": touch_ends(jax.random.randint(arg_keys[4], (REQUESTS, MAXP), 0, POOL_DEV + LAND_DEV), jax.random.fold_in(arg_keys[4], 1), 0, (POOL_DEV + LAND_DEV) - 1).astype(jnp.int32),
        "lengths": ragged(arg_keys[5], REQUESTS, MEAN_LEN * REQUESTS, MAXLEN, 2).astype(jnp.int32),
        "mig_src": draw_mig_src(jax.random.fold_in(arg_keys[8], 71), 0),
        "deal": jax.random.permutation(arg_keys[7], REQUESTS).astype(jnp.int32),
    }


theta_base = 130000.0
neg_large = -1.0e30


def rotate(values, positions):
    half = values.shape[-1] // 2
    freqs = theta_base ** (-(jnp.arange(half, dtype=jnp.float32) * 2.0 / values.shape[-1]))
    angles = positions.astype(jnp.float32)[:, None, None] * freqs[None, None, :]
    cosine = jnp.cos(angles)
    sine = jnp.sin(angles)
    first = values[..., :half]
    second = values[..., half:]
    return jnp.concatenate([first * cosine - second * sine, second * cosine + first * sine], axis=-1)


def reference(xn, w_qkv, w_out, pool, page_table, lengths, mig_src, deal):
    projected = jnp.dot(xn, w_qkv, preferred_element_type=jnp.float32)
    ordered = jnp.zeros_like(projected).at[deal].set(projected)
    ordered = ordered.reshape(REQUESTS, HEADS, 3, HEAD_DIM)
    query = rotate(ordered[:, :, 0], lengths).astype(jnp.bfloat16)
    key_new = rotate(ordered[:, :, 1], lengths).astype(jnp.bfloat16)
    value_new = ordered[:, :, 2].astype(jnp.bfloat16)
    landed = pool[mig_src]
    block_of = (jnp.arange(REQUESTS, dtype=jnp.int32) // REQ_ROW)[:, None]
    use_land = page_table >= POOL_DEV
    pool_ids = jnp.clip(block_of * POOL_DEV + page_table, 0, POOL - 1).astype(jnp.int32)
    land_ids = jnp.clip(block_of * LAND_DEV + page_table - POOL_DEV, 0, LANDING - 1).astype(jnp.int32)

    def one_request(items):
        q_one, k_one, v_one, p_ids, l_ids, l_use, length = items
        pages = jnp.where(l_use[:, None, None], landed[l_ids], pool[p_ids])
        pages = pages.reshape(MAXLEN, HEADS, 2, HEAD_DIM)
        keys = pages[:, :, 0].astype(jnp.float32)
        values = pages[:, :, 1].astype(jnp.float32)
        qf = q_one.astype(jnp.float32)
        scores = jnp.einsum("he,the->ht", qf, keys) * 0.125
        valid = jnp.arange(MAXLEN, dtype=jnp.int32)[None, :] < length
        scores = jnp.where(valid, scores, neg_large)
        score_new = jnp.sum(qf * k_one.astype(jnp.float32), axis=-1) * 0.125
        top = jnp.maximum(jnp.max(scores, axis=1), score_new)
        expo = jnp.where(valid, jnp.exp(scores - top[:, None]), 0.0)
        expo_new = jnp.exp(score_new - top)
        total = jnp.sum(expo, axis=1) + expo_new
        weights = lax.optimization_barrier(expo.astype(jnp.bfloat16)).astype(jnp.float32)
        weight_new = lax.optimization_barrier(expo_new.astype(jnp.bfloat16)).astype(jnp.float32)
        numer = jnp.einsum("ht,the->he", weights, values) + weight_new[:, None] * v_one.astype(jnp.float32)
        return (numer / total[:, None]).astype(jnp.bfloat16)

    mixed = lax.map(one_request, (query, key_new, value_new, pool_ids, land_ids, use_land, lengths))
    mixed = mixed.reshape(REQUESTS, D)[deal]
    attended = jnp.dot(mixed, w_out, preferred_element_type=jnp.float32).astype(jnp.bfloat16)
    return attended, landed
```

```python
import functools

import jax
import jax.numpy as jnp
import numpy as np
from jax import lax
from jax.experimental import pallas as pl
from jax.experimental.pallas import tpu as pltpu
from jax.sharding import PartitionSpec as P

MESH = pl.DeviceIdType.MESH
BF = jnp.bfloat16
F32 = jnp.float32
HD = 64
PAGE = 64
CHUNK = 16
THETA = 130000.0
MASKED = -1e30
START = -1e20

NN = (((1,), (0,)), ((), ()))
NT = (((1,), (1,)), ((), ()))


def dot(a, b, dims=NN):
    return lax.dot_general(a, b, dims, preferred_element_type=F32)


def iota(shape, dim):
    return lax.broadcasted_iota(jnp.int32, shape, dim)


def kernel(
    rows, cols,
    xn_ref, wqkv_ref, wout_ref, pool_ref, table_ref, lens_ref, freq_ref, deal_ref, mig_ref,
    att_ref, landed_ref,
    kv, vt, g, xall, wall, sq, rq, skv, rkv, ms, mr, ps, pr, lc0, lc1, rl, tt, mx, mxs, mxr, qpad,
    loc_sem, x_sem, w_sem, q_sem, kv_sem, ring_send, ring_recv, m_sem, a_sem,
):
    me_r = lax.axis_index("row")
    me_c = lax.axis_index("col")
    pages = pool_ref.shape[0]
    slots = landed_ref.shape[0]
    all_pages = pages + slots
    reqs = lens_ref.shape[1]
    total = deal_ref.shape[0] * deal_ref.shape[1]
    slot_rows = xn_ref.shape[0]
    half_slots = slots // 2
    far = rows // 2

    pool_copy = pltpu.make_async_copy(pool_ref, kv.at[pl.ds(0, pages)], loc_sem.at[0])
    pool_copy.start()

    barrier = pltpu.get_barrier_semaphore()

    def greet_col(o, carry):
        pl.semaphore_signal(barrier, inc=1, device_id={"col": lax.rem(me_c + o, cols)}, device_id_type=MESH)
        return carry

    def greet_row(o, carry):
        pl.semaphore_signal(barrier, inc=1, device_id={"row": lax.rem(me_r + o, rows)}, device_id_type=MESH)
        return carry

    lax.fori_loop(1, cols, greet_col, 0)
    lax.fori_loop(1, rows, greet_row, 0)
    pl.semaphore_wait(barrier, cols + rows - 2)

    def to_cols(src, dst, sems):
        def send(o, carry):
            to = lax.rem(me_c + o, cols)
            pltpu.make_async_remote_copy(
                src_ref=src(to), dst_ref=dst, send_sem=sems.at[0], recv_sem=sems.at[1],
                device_id={"col": to}, device_id_type=MESH,
            ).start()
            return carry
        lax.fori_loop(1, cols, send, 0)

    def to_rows(src, dst, sems):
        def send(o, carry):
            to = lax.rem(me_r + o, rows)
            pltpu.make_async_remote_copy(
                src_ref=src(to), dst_ref=dst, send_sem=sems.at[0], recv_sem=sems.at[1],
                device_id={"row": to}, device_id_type=MESH,
            ).start()
            return carry
        lax.fori_loop(1, rows, send, 0)

    def wait_all(buf, count, sem):
        part = buf.at[pl.ds(0, count)]
        pltpu.make_async_copy(part, part, sem).wait()

    to_cols(lambda to: xn_ref, xall.at[me_c], x_sem)
    xall[me_c] = xn_ref[...]
    to_cols(lambda to: wout_ref, wall.at[me_c], w_sem)
    wall[me_c] = wout_ref[...]

    left = lax.rem(me_r + rows - 1, rows)
    right = lax.rem(me_r + 1, rows)

    def ring_step(step):
        for sign, out, came, to in ((0, ms, mr, left), (1, ps, pr, right)):
            dist = far - step
            block = lax.rem(me_r + (rows - dist if sign == 0 else dist), rows)
            lead = 0 if sign == 0 else half_slots
            first, count = (lead, half_slots) if step == 0 else (0, slots)

            def fill(t, carry):
                src = mig_ref[block * slots + t]
                own = src // pages == me_r
                page = kv[src % pages]
                out[step, t] = page if step == 0 else jnp.where(own, page, came[step - 1, t])
                return carry

            def begin(t, carry):
                out[step, t] = kv[mig_ref[block * slots + t] % pages]
                return carry

            if step == 1:
                lax.fori_loop(lead, lead + half_slots, fill, 0)
                lax.fori_loop(half_slots - lead, slots - lead, begin, 0)
            else:
                lax.fori_loop(first, first + count, fill, 0)
            ring_copy(sign, step).start()

    def ring_copy(sign, step):
        out, came, to = (ms, mr, left) if sign == 0 else (ps, pr, right)
        lead = 0 if sign == 0 else half_slots
        part = pl.ds(lead, half_slots) if step == 0 else pl.ds(0, slots)
        return pltpu.make_async_remote_copy(
            src_ref=out.at[step, part], dst_ref=came.at[step, part],
            send_sem=ring_send.at[sign, step], recv_sem=ring_recv.at[sign, step],
            device_id={"row": to}, device_id_type=MESH,
        )

    def ring_arrive(step):
        for sign in (0, 1):
            ring_copy(sign, step).wait_recv()

    pool_copy.wait()
    ring_step(0)

    lens = lens_ref[...]
    full = lens // PAGE
    rest = (lens - full * PAGE).astype(F32)
    entries = table_ref.shape[1]
    wide = jnp.concatenate(
        [table_ref[...].astype(F32), jnp.zeros((reqs, reqs - entries), F32)], axis=1
    ) if entries < reqs else table_ref[...].astype(F32)
    turned = wide.T[:entries]
    at = iota((entries, reqs), 0)
    tt[...] = jnp.where(at < full, turned, -1.0)
    last = jnp.max(jnp.where(at == full, turned, -1.0), axis=0, keepdims=True)
    halves = 2
    per = all_pages // halves
    for part in range(halves):
        ids = (iota((per, reqs), 0) + part * per).astype(F32)

        def tally(t, count):
            return count + jnp.where(tt[pl.ds(t, 1), :] == ids, 1.0, 0.0)

        count = lax.fori_loop(0, entries, tally, jnp.zeros((per, reqs), F32))
        where = pl.ds(part * per, per)
        lc0[where, :] = jnp.where(count > 0.0, jnp.log(jnp.maximum(count, 1.0)), MASKED)
        lc1[where, :] = jnp.log(count + 1.0)
        rl[where, :] = jnp.where(last == ids, rest, 0.0)

    lanes = iota((128, 128), 1).astype(F32)
    for jb in range(total // 128):
        column = jnp.broadcast_to(deal_ref[jb : jb + 1, :].astype(F32), (128, 128)).T
        for ib in range(total // 128):
            g[jb * 128 : jb * 128 + 128, ib * 128 : ib * 128 + 128] = jnp.where(
                column == lanes + float(ib * 128), 1.0, 0.0
            ).astype(BF)

    angles = freq_ref[...] * lens.astype(F32)
    cosine = jnp.cos(angles)
    sine = jnp.sin(angles)

    width = wqkv_ref.shape[1]
    eye = jnp.where(iota((width, width), 0) == iota((width, width), 1), 1.0, 0.0).astype(BF)
    w_turned = dot(eye, wqkv_ref[...], NT).astype(BF)

    pick = jnp.where(iota((HD, 2 * HD), 0) + HD == iota((HD, 2 * HD), 1), 1.0, 0.0).astype(BF)

    def turn(c, carry):
        tokens = kv[pl.ds(c * CHUNK, CHUNK)].reshape(CHUNK * PAGE, 2 * HD)
        vt[c] = dot(pick, tokens, NT).astype(BF)
        return carry

    lax.fori_loop(0, pages // CHUNK, turn, 0)

    wait_all(xall, cols - 1, x_sem.at[1])
    projected = dot(w_turned, xall[...].reshape(total, xn_ref.shape[1]), NT).astype(BF)
    for b in range(rows):
        block = dot(projected, g[:, b * reqs : (b + 1) * reqs]).astype(BF)
        sq[b] = block[:HD]
        skv[b] = block[HD:]
    to_rows(lambda to: sq.at[to], rq.at[me_r], q_sem)
    to_rows(lambda to: skv.at[to], rkv.at[me_r], kv_sem)

    ring_arrive(0)
    ring_step(1)

    def rotate(x):
        u, w = x[: HD // 2], x[HD // 2 :]
        return jnp.concatenate([u * cosine - w * sine, w * cosine + u * sine], axis=0).astype(BF)

    wait_all(rq, rows - 1, q_sem.at[1])
    summed = sq[me_r].astype(F32)
    for o in range(1, rows):
        summed = summed + rq[lax.rem(me_r + o, rows)].astype(F32)
    query = rotate(summed)
    qpad[...] = jnp.concatenate([query * jnp.asarray(0.125, BF), jnp.zeros((HD, reqs), BF)], axis=0)

    offsets = iota((PAGE, reqs), 0).astype(F32)

    def chunk(c, carry):
        top, norm, acc = carry
        tokens = kv[pl.ds(c * CHUNK, CHUNK)].reshape(CHUNK * PAGE, 2 * HD)
        raw = dot(tokens, qpad[...])
        scores = []
        for p in range(CHUNK):
            row = pl.ds(c * CHUNK + p, 1)
            bias = jnp.where(offsets < rl[row, :], lc1[row, :], lc0[row, :])
            scores.append(raw[p * PAGE : (p + 1) * PAGE] + bias)
        scores = jnp.concatenate(scores, axis=0)
        new_top = jnp.maximum(top, jnp.max(scores, axis=0, keepdims=True))
        weights = jnp.exp(scores - new_top)
        scale = jnp.exp(top - new_top)
        norm = norm * scale + jnp.sum(weights, axis=0, keepdims=True)
        acc = acc * scale + dot(vt[c], weights.astype(BF))
        return new_top, norm, acc

    carry = (jnp.full((1, reqs), START, F32), jnp.zeros((1, reqs), F32), jnp.zeros((HD, reqs), F32))
    chunks = pages // CHUNK
    carry = lax.fori_loop(0, chunks // 2, chunk, carry)
    ring_arrive(1)
    ring_step(2)
    carry = lax.fori_loop(chunks // 2, chunks, chunk, carry)

    wait_all(rkv, rows - 1, kv_sem.at[1])
    summed = skv[me_r].astype(F32)
    for o in range(1, rows):
        summed = summed + rkv[lax.rem(me_r + o, rows)].astype(F32)
    key_new = rotate(summed[:HD])
    value_new = summed[HD:].astype(BF)

    ring_arrive(2)
    ring_step(3)

    top, norm, acc = carry
    score_new = jnp.sum(query.astype(F32) * key_new.astype(F32), axis=0, keepdims=True) * 0.125
    new_top = jnp.maximum(top, score_new)
    scale = jnp.exp(top - new_top)
    weight_new = jnp.exp(score_new - new_top)
    norm = norm * scale + weight_new
    acc = acc * scale + weight_new.astype(BF).astype(F32) * value_new.astype(F32)

    ring_arrive(3)

    def settle(t, carry):
        src = mig_ref[me_r * slots + t] // pages
        away = lax.rem(src - me_r + rows, rows)
        low = jnp.logical_or(away < far, jnp.logical_and(away == far, t < half_slots))
        kv[pages + t] = jnp.where(low, mr[far - 1, t], pr[far - 1, t])
        return carry

    lax.fori_loop(0, slots, settle, 0)
    landed_copy = pltpu.make_async_copy(kv.at[pl.ds(pages, slots)], landed_ref, loc_sem.at[1])
    landed_copy.start()
    turn(chunks, 0)
    top, norm, acc = chunk(chunks, (new_top, norm, acc))
    mixed = (acc / norm).astype(BF)

    mx[me_r] = mixed
    to_rows(lambda to: mx.at[me_r], mx.at[me_r], m_sem)
    wait_all(mx, rows - 1, m_sem.at[1])
    heads = jnp.concatenate([mx[b] for b in range(rows)], axis=1)
    odd = lax.rem(me_c, 2)
    none = jnp.zeros_like(heads)
    placed = jnp.concatenate(
        [jnp.where(odd == 0, heads, none), jnp.where(odd == 0, none, heads)], axis=0
    )
    mxs[...] = dot(g[...], placed, NT).astype(BF).reshape(mxs.shape)
    to_cols(lambda to: mxs.at[to], mxr.at[me_c], a_sem)
    mxr[me_c] = mxs[me_c]
    wait_all(wall, cols - 1, w_sem.at[1])
    wait_all(mxr, cols - 1, a_sem.at[1])
    pairs = jnp.concatenate([mxr[2 * k] + mxr[2 * k + 1] for k in range(cols // 2)], axis=1)
    att_ref[...] = dot(pairs, wall[...].reshape(cols * HD, wout_ref.shape[1])).astype(BF)

    wait_all(xall, cols - 1, x_sem.at[0])
    wait_all(wall, cols - 1, w_sem.at[0])
    wait_all(rq, rows - 1, q_sem.at[0])
    wait_all(rkv, rows - 1, kv_sem.at[0])
    wait_all(mx, rows - 1, m_sem.at[0])
    wait_all(mxr, cols - 1, a_sem.at[0])
    for step in range(far):
        for sign in (0, 1):
            ring_copy(sign, step).wait_send()
    landed_copy.wait()


def on_device(rows, cols, interpret, xn, w_qkv, w_out, pool, page_table, lengths, mig_src, deal):
    reqs = lengths.shape[0]
    pages, page, lanes = pool.shape
    slots = mig_src.shape[0] // rows
    total = deal.shape[0]
    slot_rows, depth = xn.shape
    freqs = THETA ** (-(np.arange(HD // 2, dtype=np.float64) * 2.0 / HD))
    freqs = jnp.asarray(np.repeat(freqs.astype(np.float32)[:, None], reqs, axis=1))
    vmem = pl.BlockSpec(memory_space=pltpu.VMEM)
    hbm = pl.BlockSpec(memory_space=pl.ANY)
    smem = pl.BlockSpec(memory_space=pltpu.SMEM)
    far = rows // 2
    dma = pltpu.SemaphoreType.DMA
    return pl.pallas_call(
        functools.partial(kernel, rows, cols),
        out_shape=(
            jax.ShapeDtypeStruct((slot_rows, w_out.shape[1]), BF),
            jax.ShapeDtypeStruct((slots, page, lanes), BF),
        ),
        in_specs=[vmem, vmem, vmem, hbm, vmem, vmem, vmem, vmem, smem],
        out_specs=(vmem, hbm),
        scratch_shapes=[
            pltpu.VMEM((pages + slots, page, lanes), BF),
            pltpu.VMEM(((pages + slots) // CHUNK, HD, CHUNK * page), BF),
            pltpu.VMEM((total, total), BF),
            pltpu.VMEM((cols, slot_rows, depth), BF),
            pltpu.VMEM((cols, HD, w_out.shape[1]), BF),
            pltpu.VMEM((rows, HD, reqs), BF),
            pltpu.VMEM((rows, HD, reqs), BF),
            pltpu.VMEM((rows, 2 * HD, reqs), BF),
            pltpu.VMEM((rows, 2 * HD, reqs), BF),
            pltpu.VMEM((far, slots, page, lanes), BF),
            pltpu.VMEM((far, slots, page, lanes), BF),
            pltpu.VMEM((far, slots, page, lanes), BF),
            pltpu.VMEM((far, slots, page, lanes), BF),
            pltpu.VMEM((pages + slots, reqs), F32),
            pltpu.VMEM((pages + slots, reqs), F32),
            pltpu.VMEM((pages + slots, reqs), F32),
            pltpu.VMEM((page_table.shape[1], reqs), F32),
            pltpu.VMEM((rows, HD, reqs), BF),
            pltpu.VMEM((cols, slot_rows, 2 * HD), BF),
            pltpu.VMEM((cols, slot_rows, 2 * HD), BF),
            pltpu.VMEM((2 * HD, reqs), BF),
            dma((2,)), dma((2,)), dma((2,)), dma((2,)), dma((2,)),
            dma((2, far)), dma((2, far)), dma((2,)), dma((2,)),
        ],
        compiler_params=pltpu.CompilerParams(
            collective_id=0, has_side_effects=True, vmem_limit_bytes=50 * 2**20
        ),
    )(xn, w_qkv, w_out, pool, page_table, lengths.reshape(1, reqs), freqs, deal.reshape(total // 128, 128), mig_src)


def solution(mesh):
    return jax.shard_map(
        functools.partial(on_device, mesh.shape["row"], mesh.shape["col"], False),
        mesh=mesh,
        in_specs=(
            P("col", "row"),
            P("row", "col"),
            P("col", "row"),
            P("row", None, "col"),
            P("row", None),
            P("row"),
            P(),
            P(),
        ),
        out_specs=(P("col", "row"), P("row", None, "col")),
        check_vma=False,
    )
```

```python
import functools

import jax
import jax.numpy as jnp
import numpy as np
from jax import lax
from jax.experimental import pallas as pl
from jax.experimental.pallas import tpu as pltpu
from jax.sharding import PartitionSpec as P

MESH = pl.DeviceIdType.MESH
BF = jnp.bfloat16
F32 = jnp.float32
HD = 64
PAGE = 64
CHUNK = 16
THETA = 130000.0
MASKED = -1e30
START = -1e20

NN = (((1,), (0,)), ((), ()))
NT = (((1,), (1,)), ((), ()))


def dot(a, b, dims=NN):
    return lax.dot_general(a, b, dims, preferred_element_type=F32)


def iota(shape, dim):
    return lax.broadcasted_iota(jnp.int32, shape, dim)


def kernel(
    rows, cols,
    xn_ref, wqkv_hbm, wout_ref, pool_ref, table_hbm, lens_hbm, freq_hbm, deal_hbm, mig_hbm,
    att_ref, landed_ref,
    wqkv_ref, table_ref, lens_ref, freq_ref, deal_ref, mig_ref, kv, vt, g, xall, wall, sq, rq, skv, rkv, ms, mr, ps, pr, lc0, lc1, rl, tt, mx, mxs, mxr, qpad,
    loc_sem, x_sem, w_sem, q_sem, kv_sem, ring_send, ring_recv, m_sem, a_sem,
):
    me_r = lax.axis_index("row")
    me_c = lax.axis_index("col")
    pages = pool_ref.shape[0]
    slots = landed_ref.shape[0]
    all_pages = pages + slots
    reqs = lens_ref.shape[1]
    total = deal_ref.shape[0] * deal_ref.shape[1]
    slot_rows = xn_ref.shape[0]
    half_slots = slots // 2
    far = rows // 2

    parts = 4
    pool_copies = [
        pltpu.make_async_copy(
            pool_ref.at[pl.ds(n * (pages // parts), pages // parts)],
            kv.at[pl.ds(n * (pages // parts), pages // parts)],
            loc_sem.at[10 + n],
        )
        for n in range(parts)
    ]
    small = [
        pltpu.make_async_copy(src, dst, loc_sem.at[2 + n])
        for n, (src, dst) in enumerate((
            (mig_hbm, mig_ref), (lens_hbm, lens_ref), (table_hbm, table_ref), (deal_hbm, deal_ref),
            (freq_hbm, freq_ref), (wqkv_hbm, wqkv_ref), (xn_ref, xall.at[me_c]), (wout_ref, wall.at[me_c]),
        ))
    ]
    for copy in small:
        copy.start()
    for copy in pool_copies:
        copy.start()

    barrier = pltpu.get_barrier_semaphore()

    def greet_col(o, carry):
        pl.semaphore_signal(barrier, inc=1, device_id={"col": lax.rem(me_c + o, cols)}, device_id_type=MESH)
        return carry

    def greet_row(o, carry):
        pl.semaphore_signal(barrier, inc=1, device_id={"row": lax.rem(me_r + o, rows)}, device_id_type=MESH)
        return carry

    lax.fori_loop(1, cols, greet_col, 0)
    lax.fori_loop(1, rows, greet_row, 0)
    pl.semaphore_wait(barrier, cols + rows - 2)

    def to_cols(src, dst, sems):
        def send(o, carry):
            to = lax.rem(me_c + o, cols)
            pltpu.make_async_remote_copy(
                src_ref=src(to), dst_ref=dst, send_sem=sems.at[0], recv_sem=sems.at[1],
                device_id={"col": to}, device_id_type=MESH,
            ).start()
            return carry
        lax.fori_loop(1, cols, send, 0)

    def to_rows(src, dst, sems):
        def send(o, carry):
            to = lax.rem(me_r + o, rows)
            pltpu.make_async_remote_copy(
                src_ref=src(to), dst_ref=dst, send_sem=sems.at[0], recv_sem=sems.at[1],
                device_id={"row": to}, device_id_type=MESH,
            ).start()
            return carry
        lax.fori_loop(1, rows, send, 0)

    def wait_all(buf, count, sem):
        part = buf.at[pl.ds(0, count)]
        pltpu.make_async_copy(part, part, sem).wait()

    to_cols(lambda to: xn_ref, xall.at[me_c], x_sem)

    left = lax.rem(me_r + rows - 1, rows)
    right = lax.rem(me_r + 1, rows)

    def hops(sign, half):
        return far if sign == half else far - 1

    def ring_copy(sign, half, hop):
        out, came, to = (ms, mr, left) if sign == 0 else (ps, pr, right)
        return pltpu.make_async_remote_copy(
            src_ref=out.at[half, hop], dst_ref=came.at[half, hop],
            send_sem=ring_send.at[sign, half, hop], recv_sem=ring_recv.at[sign, half, hop],
            device_id={"row": to}, device_id_type=MESH,
        )

    def ring_hop(hop, long):
        for sign in (0, 1):
            half = sign if long else 1 - sign
            out, came = (ms, mr) if sign == 0 else (ps, pr)
            dist = hops(sign, half) - hop
            block = lax.rem(me_r + (rows - dist if sign == 0 else dist), rows)
            first = block * slots + half * half_slots
            if hop > 0:
                ring_copy(sign, half, hop - 1).wait_recv()

            def fill(t, carry):
                src = mig_ref[first + t]
                page = kv[src % pages]
                if hop > 0:
                    page = jnp.where(src // pages == me_r, page, came[half, hop - 1, t])
                out[half, hop, t] = page
                return carry

            lax.fori_loop(0, half_slots, fill, 0)
            ring_copy(sign, half, hop).start()

    for copy in small:
        copy.wait()
    for copy in pool_copies:
        copy.wait()
    ring_hop(0, True)
    ring_hop(0, False)

    lens = lens_ref[...]

    lanes = iota((128, 128), 1).astype(F32)
    for jb in range(total // 128):
        column = jnp.broadcast_to(deal_ref[jb : jb + 1, :].astype(F32), (128, 128)).T
        for ib in range(total // 128):
            g[jb * 128 : jb * 128 + 128, ib * 128 : ib * 128 + 128] = jnp.where(
                column == lanes + float(ib * 128), 1.0, 0.0
            ).astype(BF)

    angles = freq_ref[...] * lens.astype(F32)
    cosine = jnp.cos(angles)
    sine = jnp.sin(angles)

    full = lens // PAGE
    rest = (lens - full * PAGE).astype(F32)
    entries = table_ref.shape[0]
    turned = table_ref[...].astype(F32)
    at = iota((entries, reqs), 0)
    tt[...] = jnp.where(at < full, turned, -1.0)
    last = jnp.max(jnp.where(at == full, turned, -1.0), axis=0, keepdims=True)
    halves = 2
    per = all_pages // halves
    for part in range(halves):
        ids = (iota((per, reqs), 0) + part * per).astype(F32)

        def tally(t, count):
            return count + jnp.where(tt[pl.ds(t, 1), :] == ids, 1.0, 0.0)

        count = lax.fori_loop(0, entries, tally, jnp.zeros((per, reqs), F32))
        where = pl.ds(part * per, per)
        lc0[where, :] = jnp.where(count > 0.0, jnp.log(jnp.maximum(count, 1.0)), MASKED)
        lc1[where, :] = jnp.log(count + 1.0)
        rl[where, :] = jnp.where(last == ids, rest, 0.0)

    ring_hop(1, True)

    pick = jnp.where(iota((HD, 2 * HD), 0) + HD == iota((HD, 2 * HD), 1), 1.0, 0.0).astype(BF)

    def turn(c, carry):
        tokens = kv[pl.ds(c * CHUNK, CHUNK)].reshape(CHUNK * PAGE, 2 * HD)
        vt[c] = dot(pick, tokens, NT).astype(BF)
        return carry

    lax.fori_loop(0, pages // CHUNK, turn, 0)

    wait_all(xall, cols - 1, x_sem.at[1])
    projected = dot(wqkv_ref[...], xall[...].reshape(total, xn_ref.shape[1]), NT).astype(BF)
    for b in range(rows):
        block = dot(projected, g[:, b * reqs : (b + 1) * reqs]).astype(BF)
        sq[b] = block[:HD]
        skv[b] = block[HD:]
    to_rows(lambda to: sq.at[to], rq.at[me_r], q_sem)
    to_rows(lambda to: skv.at[to], rkv.at[me_r], kv_sem)

    ring_hop(1, False)
    to_cols(lambda to: wout_ref, wall.at[me_c], w_sem)

    def rotate(x):
        u, w = x[: HD // 2], x[HD // 2 :]
        return jnp.concatenate([u * cosine - w * sine, w * cosine + u * sine], axis=0).astype(BF)

    wait_all(rq, rows - 1, q_sem.at[1])
    summed = sq[me_r].astype(F32)
    for o in range(1, rows):
        summed = summed + rq[lax.rem(me_r + o, rows)].astype(F32)
    query = rotate(summed)
    qpad[...] = jnp.concatenate([query * jnp.asarray(0.125, BF), jnp.zeros((HD, reqs), BF)], axis=0)

    offsets = iota((PAGE, reqs), 0).astype(F32)

    def chunk(c, carry):
        top, norm, acc = carry
        tokens = kv[pl.ds(c * CHUNK, CHUNK)].reshape(CHUNK * PAGE, 2 * HD)
        raw = dot(tokens, qpad[...])
        scores = []
        for p in range(CHUNK):
            row = pl.ds(c * CHUNK + p, 1)
            bias = jnp.where(offsets < rl[row, :], lc1[row, :], lc0[row, :])
            scores.append(raw[p * PAGE : (p + 1) * PAGE] + bias)
        scores = jnp.concatenate(scores, axis=0)
        new_top = jnp.maximum(top, jnp.max(scores, axis=0, keepdims=True))
        weights = jnp.exp(scores - new_top)
        scale = jnp.exp(top - new_top)
        norm = norm * scale + jnp.sum(weights, axis=0, keepdims=True)
        acc = acc * scale + dot(vt[c], weights.astype(BF))
        return new_top, norm, acc

    carry = (jnp.full((1, reqs), START, F32), jnp.zeros((1, reqs), F32), jnp.zeros((HD, reqs), F32))
    chunks = pages // CHUNK
    ring_hop(2, True)
    carry = lax.fori_loop(0, chunks // 2, chunk, carry)
    ring_hop(2, False)
    carry = lax.fori_loop(chunks // 2, chunks, chunk, carry)

    wait_all(rkv, rows - 1, kv_sem.at[1])
    summed = skv[me_r].astype(F32)
    for o in range(1, rows):
        summed = summed + rkv[lax.rem(me_r + o, rows)].astype(F32)
    key_new = rotate(summed[:HD])
    value_new = summed[HD:].astype(BF)

    ring_hop(3, True)

    top, norm, acc = carry
    score_new = jnp.sum(query.astype(F32) * key_new.astype(F32), axis=0, keepdims=True) * 0.125
    new_top = jnp.maximum(top, score_new)
    scale = jnp.exp(top - new_top)
    weight_new = jnp.exp(score_new - new_top)
    norm = norm * scale + weight_new
    acc = acc * scale + weight_new.astype(BF).astype(F32) * value_new.astype(F32)

    for half in (1, 0):
        for sign in (0, 1):
            side = half if sign == 0 else 1 - half
            ring_copy(sign, side, hops(sign, side) - 1).wait_recv()

    for half in (0, 1):
        def settle(t, carry):
            src = mig_ref[me_r * slots + half * half_slots + t] // pages
            away = lax.rem(src - me_r + rows, rows)
            low = away <= far if half == 0 else away < far
            kv[pages + half * half_slots + t] = jnp.where(
                low, mr[half, hops(0, half) - 1, t], pr[half, hops(1, half) - 1, t]
            )
            return carry

        lax.fori_loop(0, half_slots, settle, 0)
    landed_copy = pltpu.make_async_copy(kv.at[pl.ds(pages, slots)], landed_ref, loc_sem.at[1])
    landed_copy.start()
    turn(chunks, 0)
    top, norm, acc = chunk(chunks, (new_top, norm, acc))
    mixed = (acc / norm).astype(BF)

    mx[me_r] = mixed
    to_rows(lambda to: mx.at[me_r], mx.at[me_r], m_sem)
    wait_all(mx, rows - 1, m_sem.at[1])
    heads = jnp.concatenate([mx[b] for b in range(rows)], axis=1)
    odd = lax.rem(me_c, 2)
    none = jnp.zeros_like(heads)
    placed = jnp.concatenate(
        [jnp.where(odd == 0, heads, none), jnp.where(odd == 0, none, heads)], axis=0
    )
    mxs[...] = dot(g[...], placed, NT).astype(BF).reshape(mxs.shape)
    to_cols(lambda to: mxs.at[to], mxr.at[me_c], a_sem)
    mxr[me_c] = mxs[me_c]
    wait_all(wall, cols - 1, w_sem.at[1])
    wait_all(mxr, cols - 1, a_sem.at[1])
    pairs = jnp.concatenate([mxr[2 * k] + mxr[2 * k + 1] for k in range(cols // 2)], axis=1)
    att_ref[...] = dot(pairs, wall[...].reshape(cols * HD, wout_ref.shape[1])).astype(BF)

    wait_all(xall, cols - 1, x_sem.at[0])
    wait_all(wall, cols - 1, w_sem.at[0])
    wait_all(rq, rows - 1, q_sem.at[0])
    wait_all(rkv, rows - 1, kv_sem.at[0])
    wait_all(mx, rows - 1, m_sem.at[0])
    wait_all(mxr, cols - 1, a_sem.at[0])
    for sign in (0, 1):
        for half in (0, 1):
            for hop in range(hops(sign, half)):
                ring_copy(sign, half, hop).wait_send()
    landed_copy.wait()


def on_device(rows, cols, interpret, xn, w_qkv, w_out, pool, page_table, lengths, mig_src, deal):
    reqs = lengths.shape[0]
    pages, page, lanes = pool.shape
    slots = mig_src.shape[0] // rows
    total = deal.shape[0]
    slot_rows, depth = xn.shape
    freqs = THETA ** (-(np.arange(HD // 2, dtype=np.float64) * 2.0 / HD))
    freqs = jnp.asarray(np.repeat(freqs.astype(np.float32)[:, None], reqs, axis=1))
    vmem = pl.BlockSpec(memory_space=pltpu.VMEM)
    hbm = pl.BlockSpec(memory_space=pltpu.HBM)
    far = rows // 2
    dma = pltpu.SemaphoreType.DMA
    return pl.pallas_call(
        functools.partial(kernel, rows, cols),
        out_shape=(
            jax.ShapeDtypeStruct((slot_rows, w_out.shape[1]), BF),
            jax.ShapeDtypeStruct((slots, page, lanes), BF),
        ),
        in_specs=[hbm] * 9,
        out_specs=(vmem, pl.BlockSpec(memory_space=pl.ANY)),
        scratch_shapes=[
            pltpu.VMEM((w_qkv.shape[1], depth), BF),
            pltpu.VMEM((page_table.shape[1], reqs), jnp.int32),
            pltpu.VMEM((1, reqs), jnp.int32),
            pltpu.VMEM((HD // 2, reqs), F32),
            pltpu.VMEM((total // 128, 128), jnp.int32),
            pltpu.SMEM(mig_src.shape, jnp.int32),
            pltpu.VMEM((pages + slots, page, lanes), BF),
            pltpu.VMEM(((pages + slots) // CHUNK, HD, CHUNK * page), BF),
            pltpu.VMEM((total, total), BF),
            pltpu.VMEM((cols, slot_rows, depth), BF),
            pltpu.VMEM((cols, HD, w_out.shape[1]), BF),
            pltpu.VMEM((rows, HD, reqs), BF),
            pltpu.VMEM((rows, HD, reqs), BF),
            pltpu.VMEM((rows, 2 * HD, reqs), BF),
            pltpu.VMEM((rows, 2 * HD, reqs), BF),
            pltpu.VMEM((2, far, slots // 2, page, lanes), BF),
            pltpu.VMEM((2, far, slots // 2, page, lanes), BF),
            pltpu.VMEM((2, far, slots // 2, page, lanes), BF),
            pltpu.VMEM((2, far, slots // 2, page, lanes), BF),
            pltpu.VMEM((pages + slots, reqs), F32),
            pltpu.VMEM((pages + slots, reqs), F32),
            pltpu.VMEM((pages + slots, reqs), F32),
            pltpu.VMEM((page_table.shape[1], reqs), F32),
            pltpu.VMEM((rows, HD, reqs), BF),
            pltpu.VMEM((cols, slot_rows, 2 * HD), BF),
            pltpu.VMEM((cols, slot_rows, 2 * HD), BF),
            pltpu.VMEM((2 * HD, reqs), BF),
            dma((14,)), dma((2,)), dma((2,)), dma((2,)), dma((2,)),
            dma((2, 2, far)), dma((2, 2, far)), dma((2,)), dma((2,)),
        ],
        compiler_params=pltpu.CompilerParams(
            collective_id=0, has_side_effects=True, vmem_limit_bytes=64 * 2**20
        ),
    )(xn, w_qkv.T, w_out, pool, page_table.T, lengths.reshape(1, reqs), freqs, deal.reshape(total // 128, 128), mig_src)


def solution(mesh):
    return jax.shard_map(
        functools.partial(on_device, mesh.shape["row"], mesh.shape["col"], False),
        mesh=mesh,
        in_specs=(
            P("col", "row"),
            P("row", "col"),
            P("col", "row"),
            P("row", None, "col"),
            P("row", None),
            P("row"),
            P(),
            P(),
        ),
        out_specs=(P("col", "row"), P("row", None, "col")),
        check_vma=False,
    )
```

```python
import functools

import jax
import jax.numpy as jnp
import numpy as np
from jax import lax
from jax.experimental import pallas as pl
from jax.experimental.pallas import tpu as pltpu
from jax.sharding import PartitionSpec as P

MESH = pl.DeviceIdType.MESH
BF = jnp.bfloat16
F32 = jnp.float32
HD = 64
PAGE = 64
CHUNK = 16
THETA = 130000.0
MASKED = -1e30
START = -1e20

NN = (((1,), (0,)), ((), ()))
NT = (((1,), (1,)), ((), ()))


def dot(a, b, dims=NN):
    return lax.dot_general(a, b, dims, preferred_element_type=F32)


def iota(shape, dim):
    return lax.broadcasted_iota(jnp.int32, shape, dim)


def kernel(
    rows, cols,
    xn_ref, wqkv_hbm, wout_ref, pool_ref, table_hbm, lens_hbm, freq_hbm, deal_hbm, mig_hbm,
    att_ref, landed_ref,
    wqkv_ref, table_ref, lens_ref, freq_ref, deal_ref, mig_ref, kv, vt, g, xall, wall, sq, rq, skv, skv_out, rkv, ms, mr, ps, pr, lc0, lc1, rl, tt, mx, mxs, mxr, qpad,
    loc_sem, x_sem, w_sem, q_sem, kv_send, kv_recv, ring_send, ring_recv, m_sem, a_sem,
):
    me_r = lax.axis_index("row")
    me_c = lax.axis_index("col")
    pages = pool_ref.shape[0]
    slots = landed_ref.shape[0]
    all_pages = pages + slots
    reqs = lens_ref.shape[1]
    total = deal_ref.shape[0] * deal_ref.shape[1]
    slot_rows = xn_ref.shape[0]
    half_slots = slots // 2
    far = rows // 2

    parts = 4
    pool_copies = [
        pltpu.make_async_copy(
            pool_ref.at[pl.ds(n * (pages // parts), pages // parts)],
            kv.at[pl.ds(n * (pages // parts), pages // parts)],
            loc_sem.at[10 + n],
        )
        for n in range(parts)
    ]
    small = [
        pltpu.make_async_copy(src, dst, loc_sem.at[2 + n])
        for n, (src, dst) in enumerate((
            (mig_hbm, mig_ref), (lens_hbm, lens_ref), (table_hbm, table_ref), (deal_hbm, deal_ref),
            (freq_hbm, freq_ref), (wqkv_hbm, wqkv_ref), (xn_ref, xall.at[me_c]), (wout_ref, wall.at[me_c]),
        ))
    ]
    for copy in small:
        copy.start()
    for copy in pool_copies:
        copy.start()

    barrier = pltpu.get_barrier_semaphore()

    def greet_col(o, carry):
        pl.semaphore_signal(barrier, inc=1, device_id={"col": lax.rem(me_c + o, cols)}, device_id_type=MESH)
        return carry

    def greet_row(o, carry):
        pl.semaphore_signal(barrier, inc=1, device_id={"row": lax.rem(me_r + o, rows)}, device_id_type=MESH)
        return carry

    lax.fori_loop(1, cols, greet_col, 0)
    lax.fori_loop(1, rows, greet_row, 0)
    pl.semaphore_wait(barrier, cols + rows - 2)

    def to_cols(src, dst, sems):
        def send(o, carry):
            to = lax.rem(me_c + o, cols)
            pltpu.make_async_remote_copy(
                src_ref=src(to), dst_ref=dst, send_sem=sems.at[0], recv_sem=sems.at[1],
                device_id={"col": to}, device_id_type=MESH,
            ).start()
            return carry
        lax.fori_loop(1, cols, send, 0)

    def to_rows(src, dst, sems):
        def send(o, carry):
            to = lax.rem(me_r + o, rows)
            pltpu.make_async_remote_copy(
                src_ref=src(to), dst_ref=dst, send_sem=sems.at[0], recv_sem=sems.at[1],
                device_id={"row": to}, device_id_type=MESH,
            ).start()
            return carry
        lax.fori_loop(1, rows, send, 0)

    def wait_all(buf, count, sem):
        part = buf.at[pl.ds(0, count)]
        pltpu.make_async_copy(part, part, sem).wait()

    to_cols(lambda to: xn_ref, xall.at[me_c], x_sem)

    left = lax.rem(me_r + rows - 1, rows)
    right = lax.rem(me_r + 1, rows)

    def hops(sign, half):
        return far if sign == half else far - 1

    def ring_copy(sign, half, hop):
        out, came, to = (ms, mr, left) if sign == 0 else (ps, pr, right)
        return pltpu.make_async_remote_copy(
            src_ref=out.at[half, hop], dst_ref=came.at[half, hop],
            send_sem=ring_send.at[sign, half, hop], recv_sem=ring_recv.at[sign, half, hop],
            device_id={"row": to}, device_id_type=MESH,
        )

    def ring_hop(hop, long):
        for sign in (0, 1):
            half = sign if long else 1 - sign
            out, came = (ms, mr) if sign == 0 else (ps, pr)
            dist = hops(sign, half) - hop
            block = lax.rem(me_r + (rows - dist if sign == 0 else dist), rows)
            first = block * slots + half * half_slots
            if hop > 0:
                ring_copy(sign, half, hop - 1).wait_recv()

            def fill(t, carry):
                src = mig_ref[first + t]
                page = kv[src % pages]
                if hop > 0:
                    page = jnp.where(src // pages == me_r, page, came[half, hop - 1, t])
                out[half, hop, t] = page
                return carry

            lax.fori_loop(0, half_slots, fill, 0)
            ring_copy(sign, half, hop).start()

    def kv_copy(sign, half, hop):
        return pltpu.make_async_remote_copy(
            src_ref=skv_out.at[sign, half, hop], dst_ref=rkv.at[sign, half, hop],
            send_sem=kv_send.at[sign, half, hop], recv_sem=kv_recv.at[sign, half, hop],
            device_id={"row": left if sign == 0 else right}, device_id_type=MESH,
        )

    def kv_hop(hop):
        for sign in (0, 1):
            for half in (sign, 1 - sign):
                if hop < hops(sign, half):
                    dist = hops(sign, half) - hop
                    block = lax.rem(me_r + (rows - dist if sign == 0 else dist), rows)
                    part = skv[block, half * HD : (half + 1) * HD]
                    if hop > 0:
                        kv_copy(sign, half, hop - 1).wait_recv()
                        part = (part.astype(F32) + rkv[sign, half, hop - 1].astype(F32)).astype(BF)
                    skv_out[sign, half, hop] = part
                    kv_copy(sign, half, hop).start()

    def kv_sum(half):
        summed = skv[me_r, half * HD : (half + 1) * HD].astype(F32)
        for sign in (0, 1):
            kv_copy(sign, half, hops(sign, half) - 1).wait_recv()
            summed = summed + rkv[sign, half, hops(sign, half) - 1].astype(F32)
        return summed

    for copy in small:
        copy.wait()
    for copy in pool_copies:
        copy.wait()
    ring_hop(0, True)
    ring_hop(0, False)

    lens = lens_ref[...]

    half_rows = slot_rows // 2
    lanes = iota((128, 128), 1).astype(F32)
    for jb in range(total // 128):
        column = jnp.broadcast_to(deal_ref[jb : jb + 1, :].astype(F32), (128, 128)).T
        for ib in range(total // 128):
            hit = jnp.where(column == lanes + float(ib * 128), 1.0, 0.0).astype(BF)
            for n in range(128 // half_rows):
                at = (jb * 128 // half_rows + n) // 2 * half_rows
                g[n % 2, at : at + half_rows, ib * 128 : ib * 128 + 128] = hit[n * half_rows : (n + 1) * half_rows]

    angles = freq_ref[...] * lens.astype(F32)
    cosine = jnp.cos(angles)
    sine = jnp.sin(angles)

    full = lens // PAGE
    rest = (lens - full * PAGE).astype(F32)
    entries = table_ref.shape[0]
    turned = table_ref[...].astype(F32)
    at = iota((entries, reqs), 0)
    tt[...] = jnp.where(at < full, turned, -1.0)
    last = jnp.max(jnp.where(at == full, turned, -1.0), axis=0, keepdims=True)
    halves = 2
    per = all_pages // halves
    for part in range(halves):
        ids = (iota((per, reqs), 0) + part * per).astype(F32)

        def tally(t, count):
            return count + jnp.where(tt[pl.ds(t, 1), :] == ids, 1.0, 0.0)

        count = lax.fori_loop(0, entries, tally, jnp.zeros((per, reqs), F32))
        where = pl.ds(part * per, per)
        lc0[where, :] = jnp.where(count > 0.0, jnp.log(jnp.maximum(count, 1.0)), MASKED)
        lc1[where, :] = jnp.log(count + 1.0)
        rl[where, :] = jnp.where(last == ids, rest, 0.0)

    ring_hop(1, True)

    pick = jnp.where(iota((HD, 2 * HD), 0) + HD == iota((HD, 2 * HD), 1), 1.0, 0.0).astype(BF)

    def turn(c, carry):
        tokens = kv[pl.ds(c * CHUNK, CHUNK)].reshape(CHUNK * PAGE, 2 * HD)
        vt[c] = dot(pick, tokens, NT).astype(BF)
        return carry

    wait_all(xall, cols - 1, x_sem.at[1])
    projected = [
        dot(
            wqkv_ref[...],
            xall[:, part * half_rows : (part + 1) * half_rows].reshape(total // 2, xn_ref.shape[1]),
            NT,
        ).astype(BF)
        for part in (0, 1)
    ]
    for b in range(rows):
        cut = slice(b * reqs, (b + 1) * reqs)
        block = (dot(projected[0], g[0, :, cut]) + dot(projected[1], g[1, :, cut])).astype(BF)
        sq[b] = block[:HD]
        skv[b] = block[HD:]
    to_rows(lambda to: sq.at[to], rq.at[me_r], q_sem)
    kv_hop(0)

    ring_hop(1, False)
    to_cols(lambda to: wout_ref, wall.at[me_c], w_sem)
    lax.fori_loop(0, pages // CHUNK, turn, 0)

    def rotate(x):
        u, w = x[: HD // 2], x[HD // 2 :]
        return jnp.concatenate([u * cosine - w * sine, w * cosine + u * sine], axis=0).astype(BF)

    wait_all(rq, rows - 1, q_sem.at[1])
    summed = sq[me_r].astype(F32)
    for o in range(1, rows):
        summed = summed + rq[lax.rem(me_r + o, rows)].astype(F32)
    query = rotate(summed)
    qpad[...] = jnp.concatenate([query * jnp.asarray(0.125, BF), jnp.zeros((HD, reqs), BF)], axis=0)

    offsets = iota((PAGE, reqs), 0).astype(F32)

    def chunk(c, carry):
        top, norm, acc = carry
        tokens = kv[pl.ds(c * CHUNK, CHUNK)].reshape(CHUNK * PAGE, 2 * HD)
        raw = dot(tokens, qpad[...])
        scores = []
        for p in range(CHUNK):
            row = pl.ds(c * CHUNK + p, 1)
            bias = jnp.where(offsets < rl[row, :], lc1[row, :], lc0[row, :])
            scores.append(raw[p * PAGE : (p + 1) * PAGE] + bias)
        scores = jnp.concatenate(scores, axis=0)
        new_top = jnp.maximum(top, jnp.max(scores, axis=0, keepdims=True))
        weights = jnp.exp(scores - new_top)
        scale = jnp.exp(top - new_top)
        norm = norm * scale + jnp.sum(weights, axis=0, keepdims=True)
        acc = acc * scale + dot(vt[c], weights.astype(BF))
        return new_top, norm, acc

    carry = (jnp.full((1, reqs), START, F32), jnp.zeros((1, reqs), F32), jnp.zeros((HD, reqs), F32))
    chunks = pages // CHUNK
    kv_hop(1)
    ring_hop(2, True)
    carry = lax.fori_loop(0, chunks // 2, chunk, carry)
    kv_hop(2)
    ring_hop(2, False)
    carry = lax.fori_loop(chunks // 2, chunks, chunk, carry)

    kv_hop(3)
    ring_hop(3, True)

    key_new = rotate(kv_sum(0))
    value_new = kv_sum(1).astype(BF)
    top, norm, acc = carry
    score_new = jnp.sum(query.astype(F32) * key_new.astype(F32), axis=0, keepdims=True) * 0.125
    new_top = jnp.maximum(top, score_new)
    scale = jnp.exp(top - new_top)
    weight_new = jnp.exp(score_new - new_top)
    norm = norm * scale + weight_new
    acc = acc * scale + weight_new.astype(BF).astype(F32) * value_new.astype(F32)

    for half in (1, 0):
        for sign in (0, 1):
            side = half if sign == 0 else 1 - half
            ring_copy(sign, side, hops(sign, side) - 1).wait_recv()

    for half in (0, 1):
        def settle(t, carry):
            src = mig_ref[me_r * slots + half * half_slots + t] // pages
            away = lax.rem(src - me_r + rows, rows)
            low = away <= far if half == 0 else away < far
            kv[pages + half * half_slots + t] = jnp.where(
                low, mr[half, hops(0, half) - 1, t], pr[half, hops(1, half) - 1, t]
            )
            return carry

        lax.fori_loop(0, half_slots, settle, 0)
    landed_copy = pltpu.make_async_copy(kv.at[pl.ds(pages, slots)], landed_ref, loc_sem.at[1])
    landed_copy.start()
    turn(chunks, 0)
    top, norm, acc = chunk(chunks, (new_top, norm, acc))
    mixed = (acc / norm).astype(BF)

    mx[me_r] = mixed
    to_rows(lambda to: mx.at[me_r], mx.at[me_r], m_sem)
    wait_all(mx, rows - 1, m_sem.at[1])
    heads = jnp.concatenate([mx[b] for b in range(rows)], axis=1)
    none = jnp.zeros_like(heads)
    packed = dot(g[0], jnp.concatenate([heads, none], axis=0), NT) + dot(
        g[1], jnp.concatenate([none, heads], axis=0), NT
    )
    mxs[...] = packed.astype(BF).reshape(mxs.shape)
    to_cols(lambda to: mxs.at[to], mxr.at[me_c], a_sem)
    mxr[me_c] = mxs[me_c]
    wait_all(wall, cols - 1, w_sem.at[1])
    wait_all(mxr, cols - 1, a_sem.at[1])
    even = jnp.concatenate([mxr[2 * k] for k in range(cols // 2)], axis=0).astype(F32)
    odd = jnp.concatenate([mxr[2 * k + 1] for k in range(cols // 2)], axis=0).astype(F32)
    first = iota(even.shape, 1) < HD
    low = jnp.where(first, even, pltpu.roll(odd, HD, 1)).astype(BF)
    high = jnp.where(first, pltpu.roll(even, HD, 1), odd).astype(BF)
    pairs = jnp.concatenate(
        [
            jnp.concatenate([x[k * half_rows : (k + 1) * half_rows] for k in range(cols // 2)], axis=1)
            for x in (low, high)
        ],
        axis=0,
    )
    att_ref[...] = dot(pairs, wall[...].reshape(cols * HD, wout_ref.shape[1])).astype(BF)

    wait_all(xall, cols - 1, x_sem.at[0])
    wait_all(wall, cols - 1, w_sem.at[0])
    wait_all(rq, rows - 1, q_sem.at[0])
    wait_all(mx, rows - 1, m_sem.at[0])
    wait_all(mxr, cols - 1, a_sem.at[0])
    for sign in (0, 1):
        for half in (0, 1):
            for hop in range(hops(sign, half)):
                ring_copy(sign, half, hop).wait_send()
                kv_copy(sign, half, hop).wait_send()
    landed_copy.wait()


def on_device(rows, cols, interpret, xn, w_qkv, w_out, pool, page_table, lengths, mig_src, deal):
    reqs = lengths.shape[0]
    pages, page, lanes = pool.shape
    slots = mig_src.shape[0] // rows
    total = deal.shape[0]
    slot_rows, depth = xn.shape
    freqs = THETA ** (-(np.arange(HD // 2, dtype=np.float64) * 2.0 / HD))
    freqs = jnp.asarray(np.repeat(freqs.astype(np.float32)[:, None], reqs, axis=1))
    vmem = pl.BlockSpec(memory_space=pltpu.VMEM)
    hbm = pl.BlockSpec(memory_space=pltpu.HBM)
    far = rows // 2
    dma = pltpu.SemaphoreType.DMA
    return pl.pallas_call(
        functools.partial(kernel, rows, cols),
        out_shape=(
            jax.ShapeDtypeStruct((slot_rows, w_out.shape[1]), BF),
            jax.ShapeDtypeStruct((slots, page, lanes), BF),
        ),
        in_specs=[hbm] * 9,
        out_specs=(vmem, pl.BlockSpec(memory_space=pl.ANY)),
        scratch_shapes=[
            pltpu.VMEM((w_qkv.shape[1], depth), BF),
            pltpu.VMEM((page_table.shape[1], reqs), jnp.int32),
            pltpu.VMEM((1, reqs), jnp.int32),
            pltpu.VMEM((HD // 2, reqs), F32),
            pltpu.VMEM((total // 128, 128), jnp.int32),
            pltpu.SMEM(mig_src.shape, jnp.int32),
            pltpu.VMEM((pages + slots, page, lanes), BF),
            pltpu.VMEM(((pages + slots) // CHUNK, HD, CHUNK * page), BF),
            pltpu.VMEM((2, total // 2, total), BF),
            pltpu.VMEM((cols, slot_rows, depth), BF),
            pltpu.VMEM((cols, HD, w_out.shape[1]), BF),
            pltpu.VMEM((rows, HD, reqs), BF),
            pltpu.VMEM((rows, HD, reqs), BF),
            pltpu.VMEM((rows, 2 * HD, reqs), BF),
            pltpu.VMEM((2, 2, far, HD, reqs), BF),
            pltpu.VMEM((2, 2, far, HD, reqs), BF),
            pltpu.VMEM((2, far, slots // 2, page, lanes), BF),
            pltpu.VMEM((2, far, slots // 2, page, lanes), BF),
            pltpu.VMEM((2, far, slots // 2, page, lanes), BF),
            pltpu.VMEM((2, far, slots // 2, page, lanes), BF),
            pltpu.VMEM((pages + slots, reqs), F32),
            pltpu.VMEM((pages + slots, reqs), F32),
            pltpu.VMEM((pages + slots, reqs), F32),
            pltpu.VMEM((page_table.shape[1], reqs), F32),
            pltpu.VMEM((rows, HD, reqs), BF),
            pltpu.VMEM((cols, slot_rows // 2, 2 * HD), BF),
            pltpu.VMEM((cols, slot_rows // 2, 2 * HD), BF),
            pltpu.VMEM((2 * HD, reqs), BF),
            dma((14,)), dma((2,)), dma((2,)), dma((2,)), dma((2, 2, far)), dma((2, 2, far)),
            dma((2, 2, far)), dma((2, 2, far)), dma((2,)), dma((2,)),
        ],
        compiler_params=pltpu.CompilerParams(
            collective_id=0, has_side_effects=True, vmem_limit_bytes=64 * 2**20
        ),
    )(xn, w_qkv.T, w_out, pool, page_table.T, lengths.reshape(1, reqs), freqs, deal.reshape(total // 128, 128), mig_src)


def solution(mesh):
    return jax.shard_map(
        functools.partial(on_device, mesh.shape["row"], mesh.shape["col"], False),
        mesh=mesh,
        in_specs=(
            P("col", "row"),
            P("row", "col"),
            P("col", "row"),
            P("row", None, "col"),
            P("row", None),
            P("row"),
            P(),
            P(),
        ),
        out_specs=(P("col", "row"), P("row", None, "col")),
        check_vma=False,
    )
```

```python
import functools

import jax
import jax.numpy as jnp
import numpy as np
from jax import lax
from jax.experimental import pallas as pl
from jax.experimental.pallas import tpu as pltpu
from jax.sharding import PartitionSpec as P

MESH = pl.DeviceIdType.MESH
BF = jnp.bfloat16
F32 = jnp.float32
HD = 64
PAGE = 64
CHUNK = 16
THETA = 130000.0
MASKED = -1e30
START = -1e20

NN = (((1,), (0,)), ((), ()))
NT = (((1,), (1,)), ((), ()))


def dot(a, b, dims=NN):
    return lax.dot_general(a, b, dims, preferred_element_type=F32)


def iota(shape, dim):
    return lax.broadcasted_iota(jnp.int32, shape, dim)


def kernel(
    rows, cols,
    xn_ref, wqkv_hbm, wout_ref, pool_ref, table_hbm, lens_hbm, freq_hbm, deal_hbm, mig_hbm,
    att_ref, landed_ref,
    wqkv_ref, table_ref, lens_ref, freq_ref, deal_ref, mig_ref, kv, vt, g, xall, wall, sq, rq, skv, kv_out, rkv, ms, mr, ps, pr, lc0, lc1, rl, tt, mx, mxs, mxr, qpad,
    loc_sem, x_sem, w_sem, q_sem, kv_send, kv_recv, ring_send, ring_recv, m_sem, a_sem,
):
    me_r = lax.axis_index("row")
    me_c = lax.axis_index("col")
    pages = pool_ref.shape[0]
    slots = landed_ref.shape[0]
    all_pages = pages + slots
    reqs = lens_ref.shape[1]
    total = deal_ref.shape[0] * deal_ref.shape[1]
    slot_rows = xn_ref.shape[0]
    half_slots = slots // 2
    far = rows // 2

    parts = 4
    pool_copies = [
        pltpu.make_async_copy(
            pool_ref.at[pl.ds(n * (pages // parts), pages // parts)],
            kv.at[pl.ds(n * (pages // parts), pages // parts)],
            loc_sem.at[10 + n],
        )
        for n in range(parts)
    ]
    small = [
        pltpu.make_async_copy(src, dst, loc_sem.at[2 + n])
        for n, (src, dst) in enumerate((
            (mig_hbm, mig_ref), (lens_hbm, lens_ref), (table_hbm, table_ref), (deal_hbm, deal_ref),
            (freq_hbm, freq_ref), (wqkv_hbm, wqkv_ref), (xn_ref, xall.at[lax.rem(me_c, 2), me_c // 2]), (wout_ref, wall.at[me_c]),
        ))
    ]
    for copy in small:
        copy.start()
    for copy in pool_copies:
        copy.start()

    barrier = pltpu.get_barrier_semaphore()

    def greet_col(o, carry):
        pl.semaphore_signal(barrier, inc=1, device_id={"col": lax.rem(me_c + o, cols)}, device_id_type=MESH)
        return carry

    def greet_row(o, carry):
        pl.semaphore_signal(barrier, inc=1, device_id={"row": lax.rem(me_r + o, rows)}, device_id_type=MESH)
        return carry

    lax.fori_loop(1, cols, greet_col, 0)
    lax.fori_loop(1, rows, greet_row, 0)
    pl.semaphore_wait(barrier, cols + rows - 2)

    def to_cols(src, dst, sems):
        def send(o, carry):
            to = lax.rem(me_c + o, cols)
            pltpu.make_async_remote_copy(
                src_ref=src(to), dst_ref=dst, send_sem=sems.at[0], recv_sem=sems.at[1],
                device_id={"col": to}, device_id_type=MESH,
            ).start()
            return carry
        lax.fori_loop(1, cols, send, 0)

    def to_rows(src, dst, sems):
        def send(o, carry):
            to = lax.rem(me_r + o, rows)
            pltpu.make_async_remote_copy(
                src_ref=src(to), dst_ref=dst, send_sem=sems.at[0], recv_sem=sems.at[1],
                device_id={"row": to}, device_id_type=MESH,
            ).start()
            return carry
        lax.fori_loop(1, rows, send, 0)

    def wait_all(buf, count, sem):
        part = buf.at[pl.ds(0, count)]
        pltpu.make_async_copy(part, part, sem).wait()

    core = lax.rem(me_c, 2)
    chip = me_c // 2
    sibling = me_c + 1 - 2 * core

    def to_chip(o, carry):
        pltpu.make_async_remote_copy(
            src_ref=xn_ref, dst_ref=xall.at[core, chip], send_sem=x_sem.at[0], recv_sem=x_sem.at[1],
            device_id={"col": lax.rem(me_c + 2 * o, cols)}, device_id_type=MESH,
        ).start()
        return carry

    lax.fori_loop(1, cols // 2, to_chip, 0)
    x_share = pltpu.make_async_remote_copy(
        src_ref=xall.at[core], dst_ref=xall.at[core], send_sem=x_sem.at[2], recv_sem=x_sem.at[3],
        device_id={"col": sibling}, device_id_type=MESH,
    )

    left = lax.rem(me_r + rows - 1, rows)
    right = lax.rem(me_r + 1, rows)

    def hops(sign, half):
        return far if sign == half else far - 1

    def ring_copy(sign, half, hop):
        out, came, to = (ms, mr, left) if sign == 0 else (ps, pr, right)
        return pltpu.make_async_remote_copy(
            src_ref=out.at[half, hop], dst_ref=came.at[half, hop],
            send_sem=ring_send.at[sign, half, hop], recv_sem=ring_recv.at[sign, half, hop],
            device_id={"row": to}, device_id_type=MESH,
        )

    def ring_hop(hop, long):
        for sign in (0, 1):
            half = sign if long else 1 - sign
            out, came = (ms, mr) if sign == 0 else (ps, pr)
            dist = hops(sign, half) - hop
            block = lax.rem(me_r + (rows - dist if sign == 0 else dist), rows)
            first = block * slots + half * half_slots
            if hop > 0:
                ring_copy(sign, half, hop - 1).wait_recv()

            def fill(t, carry):
                src = mig_ref[first + t]
                page = kv[src % pages]
                if hop > 0:
                    page = jnp.where(src // pages == me_r, page, came[half, hop - 1, t])
                out[half, hop, t] = page
                return carry

            lax.fori_loop(0, half_slots, fill, 0)
            ring_copy(sign, half, hop).start()

    def row_at(shift):
        return lax.rem(me_r + rows + shift, rows)

    def half_of(block, half):
        return skv.at[row_at(block), pl.ds(half * HD, HD)]

    def kv_copy(half, slot):
        s = 1 - 2 * half
        block, to = ((-4, -2), (-3, -1), (3, 1), (-1, -1), (1, 1), (None, -2), (None, 2))[slot]
        return pltpu.make_async_remote_copy(
            src_ref=kv_out.at[half, slot - 5] if block is None else half_of(block * s, half),
            dst_ref=rkv.at[half, slot],
            send_sem=kv_send.at[half, slot], recv_sem=kv_recv.at[half, slot],
            device_id={"row": row_at(to * s)}, device_id_type=MESH,
        )

    def kv_first():
        for slot in range(5):
            for half in (0, 1):
                kv_copy(half, slot).start()

    def kv_second():
        for half in (0, 1):
            s = 1 - 2 * half
            for slot, side, parts in ((5, -2 * s, (0, 1)), (6, 2 * s, (2,))):
                summed = half_of(side, half)[...].astype(F32)
                for part in parts:
                    kv_copy(half, part).wait_recv()
                    summed = summed + rkv[half, part].astype(F32)
                kv_out[half, slot - 5] = summed.astype(BF)
                kv_copy(half, slot).start()

    def kv_sum(half):
        summed = half_of(0, half)[...].astype(F32)
        for slot in range(3, 7):
            kv_copy(half, slot).wait_recv()
            summed = summed + rkv[half, slot].astype(F32)
        return summed

    for copy in small:
        copy.wait()
    for copy in pool_copies:
        copy.wait()
    ring_hop(0, True)
    ring_hop(0, False)

    lens = lens_ref[...]

    half_rows = slot_rows // 2
    lanes = iota((128, 128), 1).astype(F32)
    for jb in range(total // 128):
        column = jnp.broadcast_to(deal_ref[jb : jb + 1, :].astype(F32), (128, 128)).T
        for ib in range(total // 128):
            hit = jnp.where(column == lanes + float(ib * 128), 1.0, 0.0).astype(BF)
            for n in range(128 // half_rows):
                c = (jb * 128 // half_rows + n) // 2
                at = (c % 2 * (cols // 2) + c // 2) * half_rows
                g[n % 2, at : at + half_rows, ib * 128 : ib * 128 + 128] = hit[n * half_rows : (n + 1) * half_rows]

    angles = freq_ref[...] * lens.astype(F32)
    cosine = jnp.cos(angles)
    sine = jnp.sin(angles)

    full = lens // PAGE
    rest = (lens - full * PAGE).astype(F32)
    entries = table_ref.shape[0]
    turned = table_ref[...].astype(F32)
    at = iota((entries, reqs), 0)
    tt[...] = jnp.where(at < full, turned, -1.0)
    last = jnp.max(jnp.where(at == full, turned, -1.0), axis=0, keepdims=True)
    halves = 2
    per = all_pages // halves
    for part in range(halves):
        ids = (iota((per, reqs), 0) + part * per).astype(F32)

        def tally(t, count):
            return count + jnp.where(tt[pl.ds(t, 1), :] == ids, 1.0, 0.0)

        count = lax.fori_loop(0, entries, tally, jnp.zeros((per, reqs), F32))
        where = pl.ds(part * per, per)
        lc0[where, :] = jnp.where(count > 0.0, jnp.log(jnp.maximum(count, 1.0)), MASKED)
        lc1[where, :] = jnp.log(count + 1.0)
        rl[where, :] = jnp.where(last == ids, rest, 0.0)

    pick = jnp.where(iota((HD, 2 * HD), 0) + HD == iota((HD, 2 * HD), 1), 1.0, 0.0).astype(BF)

    def turn(c, carry):
        tokens = kv[pl.ds(c * CHUNK, CHUNK)].reshape(CHUNK * PAGE, 2 * HD)
        vt[c] = dot(pick, tokens, NT).astype(BF)
        return carry

    lax.fori_loop(0, pages // CHUNK // 2, turn, 0)
    ring_hop(1, True)
    lax.fori_loop(pages // CHUNK // 2, pages // CHUNK, turn, 0)

    ring_hop(1, False)
    wait_all(xall.at[0], cols // 2 - 1, x_sem.at[1])
    x_share.start()
    x_share.wait_recv()
    projected = [
        dot(
            wqkv_ref[...],
            xall[:, :, part * half_rows : (part + 1) * half_rows].reshape(total // 2, xn_ref.shape[1]),
            NT,
        ).astype(BF)
        for part in (0, 1)
    ]
    for b in range(rows):
        cut = slice(b * reqs, (b + 1) * reqs)
        block = (dot(projected[0], g[0, :, cut]) + dot(projected[1], g[1, :, cut])).astype(BF)
        sq[b] = block[:HD]
        skv[b] = block[HD:]
    to_rows(lambda to: sq.at[to], rq.at[me_r], q_sem)
    kv_first()
    ring_hop(2, True)
    to_cols(lambda to: wout_ref, wall.at[me_c], w_sem)
    ring_hop(2, False)

    def rotate(x):
        u, w = x[: HD // 2], x[HD // 2 :]
        return jnp.concatenate([u * cosine - w * sine, w * cosine + u * sine], axis=0).astype(BF)

    wait_all(rq, rows - 1, q_sem.at[1])
    summed = sq[me_r].astype(F32)
    for o in range(1, rows):
        summed = summed + rq[lax.rem(me_r + o, rows)].astype(F32)
    query = rotate(summed)
    qpad[...] = jnp.concatenate([query * jnp.asarray(0.125, BF), jnp.zeros((HD, reqs), BF)], axis=0)

    kv_second()
    offsets = iota((PAGE, reqs), 0).astype(F32)

    def chunk(c, carry):
        top, norm, acc = carry
        tokens = kv[pl.ds(c * CHUNK, CHUNK)].reshape(CHUNK * PAGE, 2 * HD)
        raw = dot(tokens, qpad[...])
        scores = []
        for p in range(CHUNK):
            row = pl.ds(c * CHUNK + p, 1)
            bias = jnp.where(offsets < rl[row, :], lc1[row, :], lc0[row, :])
            scores.append(raw[p * PAGE : (p + 1) * PAGE] + bias)
        scores = jnp.concatenate(scores, axis=0)
        new_top = jnp.maximum(top, jnp.max(scores, axis=0, keepdims=True))
        weights = jnp.exp(scores - new_top)
        scale = jnp.exp(top - new_top)
        norm = norm * scale + jnp.sum(weights, axis=0, keepdims=True)
        acc = acc * scale + dot(vt[c], weights.astype(BF))
        return new_top, norm, acc

    carry = (jnp.full((1, reqs), START, F32), jnp.zeros((1, reqs), F32), jnp.zeros((HD, reqs), F32))
    chunks = pages // CHUNK
    carry = lax.fori_loop(0, chunks // 2, chunk, carry)
    ring_hop(3, True)
    carry = lax.fori_loop(chunks // 2, chunks, chunk, carry)

    key_new = rotate(kv_sum(0))
    value_new = kv_sum(1).astype(BF)
    top, norm, acc = carry
    score_new = jnp.sum(query.astype(F32) * key_new.astype(F32), axis=0, keepdims=True) * 0.125
    new_top = jnp.maximum(top, score_new)
    scale = jnp.exp(top - new_top)
    weight_new = jnp.exp(score_new - new_top)
    norm = norm * scale + weight_new
    acc = acc * scale + weight_new.astype(BF).astype(F32) * value_new.astype(F32)

    for half in (1, 0):
        for sign in (0, 1):
            side = half if sign == 0 else 1 - half
            ring_copy(sign, side, hops(sign, side) - 1).wait_recv()

    for half in (0, 1):
        def settle(t, carry):
            src = mig_ref[me_r * slots + half * half_slots + t] // pages
            away = lax.rem(src - me_r + rows, rows)
            low = away <= far if half == 0 else away < far
            kv[pages + half * half_slots + t] = jnp.where(
                low, mr[half, hops(0, half) - 1, t], pr[half, hops(1, half) - 1, t]
            )
            return carry

        lax.fori_loop(0, half_slots, settle, 0)
    landed_copy = pltpu.make_async_copy(kv.at[pl.ds(pages, slots)], landed_ref, loc_sem.at[1])
    landed_copy.start()
    turn(chunks, 0)
    top, norm, acc = chunk(chunks, (new_top, norm, acc))
    mixed = (acc / norm).astype(BF)

    mx[me_r] = mixed
    to_rows(lambda to: mx.at[me_r], mx.at[me_r], m_sem)
    wait_all(mx, rows - 1, m_sem.at[1])
    heads = jnp.concatenate([mx[b] for b in range(rows)], axis=1)
    none = jnp.zeros_like(heads)
    packed = dot(g[0], jnp.concatenate([heads, none], axis=0), NT) + dot(
        g[1], jnp.concatenate([none, heads], axis=0), NT
    )
    mxs[...] = packed.astype(BF).reshape(mxs.shape)
    to_cols(lambda to: mxs.at[lax.rem(to, 2) * (cols // 2) + to // 2], mxr.at[me_c], a_sem)
    mxr[me_c] = mxs[core * (cols // 2) + chip]
    wait_all(wall, cols - 1, w_sem.at[1])
    wait_all(mxr, cols - 1, a_sem.at[1])
    even = jnp.concatenate([mxr[2 * k] for k in range(cols // 2)], axis=0).astype(F32)
    odd = jnp.concatenate([mxr[2 * k + 1] for k in range(cols // 2)], axis=0).astype(F32)
    first = iota(even.shape, 1) < HD
    low = jnp.where(first, even, pltpu.roll(odd, HD, 1)).astype(BF)
    high = jnp.where(first, pltpu.roll(even, HD, 1), odd).astype(BF)
    pairs = jnp.concatenate(
        [
            jnp.concatenate([x[k * half_rows : (k + 1) * half_rows] for k in range(cols // 2)], axis=1)
            for x in (low, high)
        ],
        axis=0,
    )
    att_ref[...] = dot(pairs, wall[...].reshape(cols * HD, wout_ref.shape[1])).astype(BF)

    wait_all(xall.at[0], cols // 2 - 1, x_sem.at[0])
    x_share.wait_send()
    wait_all(wall, cols - 1, w_sem.at[0])
    wait_all(rq, rows - 1, q_sem.at[0])
    wait_all(mx, rows - 1, m_sem.at[0])
    wait_all(mxr, cols - 1, a_sem.at[0])
    for sign in (0, 1):
        for half in (0, 1):
            for hop in range(hops(sign, half)):
                ring_copy(sign, half, hop).wait_send()
    for half in (0, 1):
        for slot in range(7):
            kv_copy(half, slot).wait_send()
    landed_copy.wait()


def on_device(rows, cols, xn, w_qkv, w_out, pool, page_table, lengths, mig_src, deal):
    reqs = lengths.shape[0]
    pages, page, lanes = pool.shape
    slots = mig_src.shape[0] // rows
    total = deal.shape[0]
    slot_rows, depth = xn.shape
    freqs = THETA ** (-(np.arange(HD // 2, dtype=np.float64) * 2.0 / HD))
    freqs = jnp.asarray(np.repeat(freqs.astype(np.float32)[:, None], reqs, axis=1))
    vmem = pl.BlockSpec(memory_space=pltpu.VMEM)
    hbm = pl.BlockSpec(memory_space=pltpu.HBM)
    far = rows // 2
    dma = pltpu.SemaphoreType.DMA
    return pl.pallas_call(
        functools.partial(kernel, rows, cols),
        out_shape=(
            jax.ShapeDtypeStruct((slot_rows, w_out.shape[1]), BF),
            jax.ShapeDtypeStruct((slots, page, lanes), BF),
        ),
        in_specs=[hbm] * 9,
        out_specs=(vmem, pl.BlockSpec(memory_space=pl.ANY)),
        scratch_shapes=[
            pltpu.VMEM((w_qkv.shape[1], depth), BF),
            pltpu.VMEM((page_table.shape[1], reqs), jnp.int32),
            pltpu.VMEM((1, reqs), jnp.int32),
            pltpu.VMEM((HD // 2, reqs), F32),
            pltpu.VMEM((total // 128, 128), jnp.int32),
            pltpu.SMEM(mig_src.shape, jnp.int32),
            pltpu.VMEM((pages + slots, page, lanes), BF),
            pltpu.VMEM(((pages + slots) // CHUNK, HD, CHUNK * page), BF),
            pltpu.VMEM((2, total // 2, total), BF),
            pltpu.VMEM((2, cols // 2, slot_rows, depth), BF),
            pltpu.VMEM((cols, HD, w_out.shape[1]), BF),
            pltpu.VMEM((rows, HD, reqs), BF),
            pltpu.VMEM((rows, HD, reqs), BF),
            pltpu.VMEM((rows, 2 * HD, reqs), BF),
            pltpu.VMEM((2, 2, HD, reqs), BF),
            pltpu.VMEM((2, 7, HD, reqs), BF),
            pltpu.VMEM((2, far, slots // 2, page, lanes), BF),
            pltpu.VMEM((2, far, slots // 2, page, lanes), BF),
            pltpu.VMEM((2, far, slots // 2, page, lanes), BF),
            pltpu.VMEM((2, far, slots // 2, page, lanes), BF),
            pltpu.VMEM((pages + slots, reqs), F32),
            pltpu.VMEM((pages + slots, reqs), F32),
            pltpu.VMEM((pages + slots, reqs), F32),
            pltpu.VMEM((page_table.shape[1], reqs), F32),
            pltpu.VMEM((rows, HD, reqs), BF),
            pltpu.VMEM((cols, slot_rows // 2, 2 * HD), BF),
            pltpu.VMEM((cols, slot_rows // 2, 2 * HD), BF),
            pltpu.VMEM((2 * HD, reqs), BF),
            dma((14,)), dma((4,)), dma((2,)), dma((2,)), dma((2, 7)), dma((2, 7)),
            dma((2, 2, far)), dma((2, 2, far)), dma((2,)), dma((2,)),
        ],
        compiler_params=pltpu.CompilerParams(
            collective_id=0, has_side_effects=True, vmem_limit_bytes=64 * 2**20
        ),
    )(xn, w_qkv.T, w_out, pool, page_table.T, lengths.reshape(1, reqs), freqs, deal.reshape(total // 128, 128), mig_src)


def solution(mesh):
    return jax.shard_map(
        functools.partial(on_device, mesh.shape["row"], mesh.shape["col"]),
        mesh=mesh,
        in_specs=(
            P("col", "row"),
            P("row", "col"),
            P("col", "row"),
            P("row", None, "col"),
            P("row", None),
            P("row"),
            P(),
            P(),
        ),
        out_specs=(P("col", "row"), P("row", None, "col")),
        check_vma=False,
    )
```

```python
import functools

import jax
import jax.numpy as jnp
import numpy as np
from jax import lax
from jax.experimental import pallas as pl
from jax.experimental.pallas import tpu as pltpu
from jax.sharding import PartitionSpec as P

MESH = pl.DeviceIdType.MESH
BF = jnp.bfloat16
F32 = jnp.float32
HD = 64
PAGE = 64
CHUNK = 16
THETA = 130000.0
MASKED = -1e30
START = -1e20

NN = (((1,), (0,)), ((), ()))
NT = (((1,), (1,)), ((), ()))


def dot(a, b, dims=NN):
    return lax.dot_general(a, b, dims, preferred_element_type=F32)


def iota(shape, dim):
    return lax.broadcasted_iota(jnp.int32, shape, dim)


def kernel(
    rows, cols,
    xn_ref, wqkv_hbm, wout_ref, pool_ref, table_hbm, lens_hbm, freq_hbm, deal_hbm, mig_hbm,
    att_ref, landed_ref,
    wqkv_ref, table_ref, lens_ref, freq_ref, deal_ref, mig_ref, kv, vt, g, xall, wall, sq, rq, skv, kv_out, rkv, ms, mr, ps, pr, lc0, lc1, rl, tt, mx, mxs, mxr, qpad,
    loc_sem, x_sem, w_sem, q_sem, kv_send, kv_recv, ring_send, ring_recv, m_sem, a_sem,
):
    me_r = lax.axis_index("row")
    me_c = lax.axis_index("col")
    pages = pool_ref.shape[0]
    slots = landed_ref.shape[0]
    all_pages = pages + slots
    reqs = lens_ref.shape[1]
    total = deal_ref.shape[0] * deal_ref.shape[1]
    slot_rows = xn_ref.shape[0]
    half_slots = slots // 2
    far = rows // 2

    parts = 4
    pool_copies = [
        pltpu.make_async_copy(
            pool_ref.at[pl.ds(n * (pages // parts), pages // parts)],
            kv.at[pl.ds(n * (pages // parts), pages // parts)],
            loc_sem.at[10 + n],
        )
        for n in range(parts)
    ]
    small = [
        pltpu.make_async_copy(src, dst, loc_sem.at[2 + n])
        for n, (src, dst) in enumerate((
            (mig_hbm, mig_ref), (lens_hbm, lens_ref), (table_hbm, table_ref), (deal_hbm, deal_ref),
            (freq_hbm, freq_ref), (wqkv_hbm, wqkv_ref), (xn_ref, xall.at[lax.rem(me_c, 2), me_c // 2]), (wout_ref, wall.at[lax.rem(me_c, 2), me_c // 2]),
        ))
    ]
    for copy in small:
        copy.start()
    for copy in pool_copies:
        copy.start()

    barrier = pltpu.get_barrier_semaphore()

    def greet_col(o, carry):
        pl.semaphore_signal(barrier, inc=1, device_id={"col": lax.rem(me_c + o, cols)}, device_id_type=MESH)
        return carry

    def greet_row(o, carry):
        pl.semaphore_signal(barrier, inc=1, device_id={"row": lax.rem(me_r + o, rows)}, device_id_type=MESH)
        return carry

    lax.fori_loop(1, cols, greet_col, 0, unroll=True)
    lax.fori_loop(1, rows, greet_row, 0, unroll=True)
    pl.semaphore_wait(barrier, cols + rows - 2)

    def to_cols(src, dst, sems):
        def send(o, carry):
            to = lax.rem(me_c + o, cols)
            pltpu.make_async_remote_copy(
                src_ref=src(to), dst_ref=dst, send_sem=sems.at[0], recv_sem=sems.at[1],
                device_id={"col": to}, device_id_type=MESH,
            ).start()
            return carry
        lax.fori_loop(1, cols, send, 0, unroll=True)

    def to_rows(src, dst, sems):
        def send(o, carry):
            to = lax.rem(me_r + o, rows)
            pltpu.make_async_remote_copy(
                src_ref=src(to), dst_ref=dst, send_sem=sems.at[0], recv_sem=sems.at[1],
                device_id={"row": to}, device_id_type=MESH,
            ).start()
            return carry
        lax.fori_loop(1, rows, send, 0, unroll=True)

    def wait_all(buf, count, sem):
        part = buf.at[pl.ds(0, count)]
        pltpu.make_async_copy(part, part, sem).wait()

    core = lax.rem(me_c, 2)
    chip = me_c // 2
    sibling = me_c + 1 - 2 * core

    def to_chips(src, buf, sems):
        def send(o, carry):
            pltpu.make_async_remote_copy(
                src_ref=src, dst_ref=buf.at[core, chip], send_sem=sems.at[0], recv_sem=sems.at[1],
                device_id={"col": lax.rem(me_c + 2 * o, cols)}, device_id_type=MESH,
            ).start()
            return carry
        lax.fori_loop(1, cols // 2, send, 0, unroll=True)

    def share(buf, sems):
        return pltpu.make_async_remote_copy(
            src_ref=buf.at[core], dst_ref=buf.at[core], send_sem=sems.at[2], recv_sem=sems.at[3],
            device_id={"col": sibling}, device_id_type=MESH,
        )

    to_chips(xn_ref, xall, x_sem)
    x_share = share(xall, x_sem)
    w_share = share(wall, w_sem)

    left = lax.rem(me_r + rows - 1, rows)
    right = lax.rem(me_r + 1, rows)

    def hops(sign, half):
        return far if sign == half else far - 1

    def ring_copy(sign, half, hop):
        out, came, to = (ms, mr, left) if sign == 0 else (ps, pr, right)
        return pltpu.make_async_remote_copy(
            src_ref=out.at[half, hop], dst_ref=came.at[half, hop],
            send_sem=ring_send.at[sign, half, hop], recv_sem=ring_recv.at[sign, half, hop],
            device_id={"row": to}, device_id_type=MESH,
        )

    def ring_hop(hop, long):
        for sign in (0, 1):
            half = sign if long else 1 - sign
            out, came = (ms, mr) if sign == 0 else (ps, pr)
            dist = hops(sign, half) - hop
            block = lax.rem(me_r + (rows - dist if sign == 0 else dist), rows)
            first = block * slots + half * half_slots
            if hop > 0:
                ring_copy(sign, half, hop - 1).wait_recv()

            def fill(t, carry):
                src = mig_ref[first + t]
                page = kv[src % pages]
                if hop > 0:
                    page = jnp.where(src // pages == me_r, page, came[half, hop - 1, t])
                out[half, hop, t] = page
                return carry

            lax.fori_loop(0, half_slots, fill, 0, unroll=True)
            ring_copy(sign, half, hop).start()

    def row_at(shift):
        return lax.rem(me_r + rows + shift, rows)

    def half_of(block, half):
        return skv.at[row_at(block), pl.ds(half * HD, HD)]

    def kv_copy(half, slot):
        s = 1 - 2 * half
        block, to = ((-4, -2), (-3, -1), (3, 1), (-1, -1), (1, 1), (None, -2), (None, 2))[slot]
        return pltpu.make_async_remote_copy(
            src_ref=kv_out.at[half, slot - 5] if block is None else half_of(block * s, half),
            dst_ref=rkv.at[half, slot],
            send_sem=kv_send.at[half, slot], recv_sem=kv_recv.at[half, slot],
            device_id={"row": row_at(to * s)}, device_id_type=MESH,
        )

    def kv_first():
        for slot in range(5):
            for half in (0, 1):
                kv_copy(half, slot).start()

    def kv_second():
        for half in (0, 1):
            s = 1 - 2 * half
            for slot, side, parts in ((5, -2 * s, (0, 1)), (6, 2 * s, (2,))):
                summed = half_of(side, half)[...].astype(F32)
                for part in parts:
                    kv_copy(half, part).wait_recv()
                    summed = summed + rkv[half, part].astype(F32)
                kv_out[half, slot - 5] = summed.astype(BF)
                kv_copy(half, slot).start()

    def kv_sum(half):
        summed = half_of(0, half)[...].astype(F32)
        for slot in range(3, 7):
            kv_copy(half, slot).wait_recv()
            summed = summed + rkv[half, slot].astype(F32)
        return summed

    for copy in small:
        copy.wait()
    for copy in pool_copies:
        copy.wait()
    ring_hop(0, True)
    ring_hop(0, False)

    lens = lens_ref[...]

    half_rows = slot_rows // 2
    lanes = iota((128, 128), 1).astype(F32)
    for jb in range(total // 128):
        column = jnp.broadcast_to(deal_ref[jb : jb + 1, :].astype(F32), (128, 128)).T
        for ib in range(total // 128):
            hit = jnp.where(column == lanes + float(ib * 128), 1.0, 0.0).astype(BF)
            for n in range(128 // half_rows):
                c = (jb * 128 // half_rows + n) // 2
                at = (c % 2 * (cols // 2) + c // 2) * half_rows
                g[n % 2, at : at + half_rows, ib * 128 : ib * 128 + 128] = hit[n * half_rows : (n + 1) * half_rows]

    angles = freq_ref[...] * lens.astype(F32)
    cosine = jnp.cos(angles)
    sine = jnp.sin(angles)

    full = lens // PAGE
    rest = (lens - full * PAGE).astype(F32)
    entries = table_ref.shape[0]
    turned = table_ref[...].astype(F32)
    at = iota((entries, reqs), 0)
    tt[...] = jnp.where(at < full, turned, -1.0)
    last = jnp.max(jnp.where(at == full, turned, -1.0), axis=0, keepdims=True)
    halves = 2
    per = all_pages // halves
    for part in range(halves):
        ids = (iota((per, reqs), 0) + part * per).astype(F32)

        def tally(t, count):
            return count + jnp.where(tt[pl.ds(t, 1), :] == ids, 1.0, 0.0)

        count = lax.fori_loop(0, entries, tally, jnp.zeros((per, reqs), F32))
        where = pl.ds(part * per, per)
        lc0[where, :] = jnp.where(count > 0.0, jnp.log(jnp.maximum(count, 1.0)), MASKED)
        lc1[where, :] = jnp.log(count + 1.0)
        rl[where, :] = jnp.where(last == ids, rest, 0.0)

    pick = jnp.where(iota((HD, 2 * HD), 0) + HD == iota((HD, 2 * HD), 1), 1.0, 0.0).astype(BF)

    def turn(c, carry):
        tokens = kv[pl.ds(c * CHUNK, CHUNK)].reshape(CHUNK * PAGE, 2 * HD)
        vt[c] = dot(pick, tokens, NT).astype(BF)
        return carry

    lax.fori_loop(0, pages // CHUNK // 2, turn, 0)
    ring_hop(1, True)
    lax.fori_loop(pages // CHUNK // 2, pages // CHUNK, turn, 0)

    ring_hop(1, False)
    wait_all(xall.at[0], cols // 2 - 1, x_sem.at[1])
    x_share.start()
    x_share.wait_recv()
    projected = [
        dot(
            wqkv_ref[...],
            xall[:, :, part * half_rows : (part + 1) * half_rows].reshape(total // 2, xn_ref.shape[1]),
            NT,
        ).astype(BF)
        for part in (0, 1)
    ]
    for b in range(rows):
        cut = slice(b * reqs, (b + 1) * reqs)
        block = (dot(projected[0], g[0, :, cut]) + dot(projected[1], g[1, :, cut])).astype(BF)
        sq[b] = block[:HD]
        skv[b] = block[HD:]
    to_rows(lambda to: sq.at[to], rq.at[me_r], q_sem)
    kv_first()
    ring_hop(2, True)
    to_chips(wout_ref, wall, w_sem)
    ring_hop(2, False)

    def rotate(x):
        u, w = x[: HD // 2], x[HD // 2 :]
        return jnp.concatenate([u * cosine - w * sine, w * cosine + u * sine], axis=0).astype(BF)

    wait_all(rq, rows - 1, q_sem.at[1])
    summed = sq[me_r].astype(F32)
    for o in range(1, rows):
        summed = summed + rq[lax.rem(me_r + o, rows)].astype(F32)
    query = rotate(summed)
    qpad[...] = jnp.concatenate([query * jnp.asarray(0.125, BF), jnp.zeros((HD, reqs), BF)], axis=0)

    kv_second()
    offsets = iota((PAGE, reqs), 0).astype(F32)

    def chunk(c, carry):
        top, norm, acc = carry
        tokens = kv[pl.ds(c * CHUNK, CHUNK)].reshape(CHUNK * PAGE, 2 * HD)
        raw = dot(tokens, qpad[...])
        scores = []
        for p in range(CHUNK):
            row = pl.ds(c * CHUNK + p, 1)
            bias = jnp.where(offsets < rl[row, :], lc1[row, :], lc0[row, :])
            scores.append(raw[p * PAGE : (p + 1) * PAGE] + bias)
        scores = jnp.concatenate(scores, axis=0)
        new_top = jnp.maximum(top, jnp.max(scores, axis=0, keepdims=True))
        weights = jnp.exp(scores - new_top)
        scale = jnp.exp(top - new_top)
        norm = norm * scale + jnp.sum(weights, axis=0, keepdims=True)
        acc = acc * scale + dot(vt[c], weights.astype(BF))
        return new_top, norm, acc

    carry = (jnp.full((1, reqs), START, F32), jnp.zeros((1, reqs), F32), jnp.zeros((HD, reqs), F32))
    chunks = pages // CHUNK
    carry = lax.fori_loop(0, chunks // 2, chunk, carry)
    ring_hop(3, True)
    carry = lax.fori_loop(chunks // 2, chunks, chunk, carry)

    key_new = rotate(kv_sum(0))
    value_new = kv_sum(1).astype(BF)
    top, norm, acc = carry
    score_new = jnp.sum(query.astype(F32) * key_new.astype(F32), axis=0, keepdims=True) * 0.125
    new_top = jnp.maximum(top, score_new)
    scale = jnp.exp(top - new_top)
    weight_new = jnp.exp(score_new - new_top)
    norm = norm * scale + weight_new
    acc = acc * scale + weight_new.astype(BF).astype(F32) * value_new.astype(F32)

    wait_all(wall.at[0], cols // 2 - 1, w_sem.at[1])
    w_share.start()
    for half in (1, 0):
        for sign in (0, 1):
            side = half if sign == 0 else 1 - half
            ring_copy(sign, side, hops(sign, side) - 1).wait_recv()

    for half in (0, 1):
        def settle(t, carry):
            src = mig_ref[me_r * slots + half * half_slots + t] // pages
            away = lax.rem(src - me_r + rows, rows)
            low = away <= far if half == 0 else away < far
            kv[pages + half * half_slots + t] = jnp.where(
                low, mr[half, hops(0, half) - 1, t], pr[half, hops(1, half) - 1, t]
            )
            return carry

        lax.fori_loop(0, half_slots, settle, 0)
    landed_copy = pltpu.make_async_copy(kv.at[pl.ds(pages, slots)], landed_ref, loc_sem.at[1])
    landed_copy.start()
    turn(chunks, 0)
    top, norm, acc = chunk(chunks, (new_top, norm, acc))
    mixed = (acc / norm).astype(BF)

    mx[me_r] = mixed
    to_rows(lambda to: mx.at[me_r], mx.at[me_r], m_sem)
    wait_all(mx, rows - 1, m_sem.at[1])
    heads = jnp.concatenate([mx[b] for b in range(rows)], axis=1)
    none = jnp.zeros_like(heads)
    packed = dot(g[0], jnp.concatenate([heads, none], axis=0), NT) + dot(
        g[1], jnp.concatenate([none, heads], axis=0), NT
    )
    mxs[...] = packed.astype(BF).reshape(mxs.shape)
    to_cols(lambda to: mxs.at[lax.rem(to, 2) * (cols // 2) + to // 2], mxr.at[me_c], a_sem)
    mxr[me_c] = mxs[core * (cols // 2) + chip]
    w_share.wait_recv()
    wait_all(mxr, cols - 1, a_sem.at[1])
    order = [2 * n + side for side in (0, 1) for n in range(cols // 2)]
    even = jnp.concatenate([mxr[c] for c in order[0::2]], axis=0).astype(F32)
    odd = jnp.concatenate([mxr[c] for c in order[1::2]], axis=0).astype(F32)
    first = iota(even.shape, 1) < HD
    low = jnp.where(first, even, pltpu.roll(odd, HD, 1)).astype(BF)
    high = jnp.where(first, pltpu.roll(even, HD, 1), odd).astype(BF)
    pairs = jnp.concatenate(
        [
            jnp.concatenate([x[k * half_rows : (k + 1) * half_rows] for k in range(cols // 2)], axis=1)
            for x in (low, high)
        ],
        axis=0,
    )
    att_ref[...] = dot(pairs, wall[...].reshape(cols * HD, wout_ref.shape[1])).astype(BF)

    wait_all(xall.at[0], cols // 2 - 1, x_sem.at[0])
    x_share.wait_send()
    wait_all(wall.at[0], cols // 2 - 1, w_sem.at[0])
    w_share.wait_send()
    wait_all(rq, rows - 1, q_sem.at[0])
    wait_all(mx, rows - 1, m_sem.at[0])
    wait_all(mxr, cols - 1, a_sem.at[0])
    for sign in (0, 1):
        for half in (0, 1):
            for hop in range(hops(sign, half)):
                ring_copy(sign, half, hop).wait_send()
    for half in (0, 1):
        for slot in range(7):
            kv_copy(half, slot).wait_send()
    landed_copy.wait()


def on_device(rows, cols, xn, w_qkv, w_out, pool, page_table, lengths, mig_src, deal):
    reqs = lengths.shape[0]
    pages, page, lanes = pool.shape
    slots = mig_src.shape[0] // rows
    total = deal.shape[0]
    slot_rows, depth = xn.shape
    freqs = THETA ** (-(np.arange(HD // 2, dtype=np.float64) * 2.0 / HD))
    freqs = jnp.asarray(np.repeat(freqs.astype(np.float32)[:, None], reqs, axis=1))
    vmem = pl.BlockSpec(memory_space=pltpu.VMEM)
    hbm = pl.BlockSpec(memory_space=pltpu.HBM)
    far = rows // 2
    dma = pltpu.SemaphoreType.DMA
    return pl.pallas_call(
        functools.partial(kernel, rows, cols),
        out_shape=(
            jax.ShapeDtypeStruct((slot_rows, w_out.shape[1]), BF),
            jax.ShapeDtypeStruct((slots, page, lanes), BF),
        ),
        in_specs=[hbm] * 9,
        out_specs=(vmem, pl.BlockSpec(memory_space=pl.ANY)),
        scratch_shapes=[
            pltpu.VMEM((w_qkv.shape[1], depth), BF),
            pltpu.VMEM((page_table.shape[1], reqs), jnp.int32),
            pltpu.VMEM((1, reqs), jnp.int32),
            pltpu.VMEM((HD // 2, reqs), F32),
            pltpu.VMEM((total // 128, 128), jnp.int32),
            pltpu.SMEM(mig_src.shape, jnp.int32),
            pltpu.VMEM((pages + slots, page, lanes), BF),
            pltpu.VMEM(((pages + slots) // CHUNK, HD, CHUNK * page), BF),
            pltpu.VMEM((2, total // 2, total), BF),
            pltpu.VMEM((2, cols // 2, slot_rows, depth), BF),
            pltpu.VMEM((2, cols // 2, HD, w_out.shape[1]), BF),
            pltpu.VMEM((rows, HD, reqs), BF),
            pltpu.VMEM((rows, HD, reqs), BF),
            pltpu.VMEM((rows, 2 * HD, reqs), BF),
            pltpu.VMEM((2, 2, HD, reqs), BF),
            pltpu.VMEM((2, 7, HD, reqs), BF),
            pltpu.VMEM((2, far, slots // 2, page, lanes), BF),
            pltpu.VMEM((2, far, slots // 2, page, lanes), BF),
            pltpu.VMEM((2, far, slots // 2, page, lanes), BF),
            pltpu.VMEM((2, far, slots // 2, page, lanes), BF),
            pltpu.VMEM((pages + slots, reqs), F32),
            pltpu.VMEM((pages + slots, reqs), F32),
            pltpu.VMEM((pages + slots, reqs), F32),
            pltpu.VMEM((page_table.shape[1], reqs), F32),
            pltpu.VMEM((rows, HD, reqs), BF),
            pltpu.VMEM((cols, slot_rows // 2, 2 * HD), BF),
            pltpu.VMEM((cols, slot_rows // 2, 2 * HD), BF),
            pltpu.VMEM((2 * HD, reqs), BF),
            dma((14,)), dma((4,)), dma((4,)), dma((2,)), dma((2, 7)), dma((2, 7)),
            dma((2, 2, far)), dma((2, 2, far)), dma((2,)), dma((2,)),
        ],
        compiler_params=pltpu.CompilerParams(
            collective_id=0, has_side_effects=True, vmem_limit_bytes=64 * 2**20
        ),
    )(xn, w_qkv.T, w_out, pool, page_table.T, lengths.reshape(1, reqs), freqs, deal.reshape(total // 128, 128), mig_src)


def solution(mesh):
    return jax.shard_map(
        functools.partial(on_device, mesh.shape["row"], mesh.shape["col"]),
        mesh=mesh,
        in_specs=(
            P("col", "row"),
            P("row", "col"),
            P("col", "row"),
            P("row", None, "col"),
            P("row", None),
            P("row"),
            P(),
            P(),
        ),
        out_specs=(P("col", "row"), P("row", None, "col")),
        check_vma=False,
    )
```
